128 devices in a mesh: row: 4 (over y_hi, core), col: 32 (over x, z, y_lo).
Axes of the slice: x: 4, y: 4 (y_hi: 2, y_lo: 2; y = y_hi * 2 + y_lo), z: 4, core: 2. Of those that a mesh axis runs over, the one named last changes fastest.
Arguments:
- pair: bfloat16 [768, 768, 128], P('row', 'col'), may hold values from -6 to 6
- norm_in: float32 [2, 128], replicated, may hold values from 0.1 to 1.9
- proj_weight: bfloat16 [2, 128, 512], replicated, may hold values from -0.5 to 0.5
- gate_weight: bfloat16 [2, 128, 128], replicated, may hold values from -0.5 to 0.5
- norm_out: float32 [2, 128], replicated, may hold values from 0.1 to 1.9
- out_weight: bfloat16 [2, 128, 128], replicated, may hold values from -0.5 to 0.5
Outputs:
- updated_pair: bfloat16 [768, 768, 128], P('row', 'col')
The draws below stay inside these ranges and needn't reach their ends.
All inputs are finite; a program needn't handle non-finite values.
Results may differ from the reference program's by a relative error of at most 0.018.
Values may be sent and summed in bfloat16 or wider, within the bound.
A program may use at most 64 MiB of HBM per device.

```python
import jax
import jax.numpy as jnp
from jax import lax

C = 128
CH = 128
N = 768


def steps_of(rng, shape, cuts, smallest, top_value):
    def one(dim, parts):
        steps = jax.random.uniform(jax.random.fold_in(jax.random.fold_in(rng, 6), dim), (parts,), jnp.float32, smallest / len(cuts), top_value / len(cuts))
        return jnp.repeat(jnp.exp(steps), shape[dim] // parts).reshape((-1,) + (1,) * (len(shape) - dim - 1))

    loudness = one(*cuts[0])
    for cut in cuts[1:]:
        loudness = loudness * one(*cut)
    return loudness


def normal_values(rng, dims, scale, reach, pieces=(), dtype=jnp.bfloat16):
    values = jax.random.normal(rng, dims, jnp.float32) * scale
    if len(pieces) > 0:
        values = steps_of(rng, dims, pieces, -0.22, 0.18) * values
    return jnp.clip(values, min=-reach, max=reach).astype(dtype)


def setup_inputs(seed: int = 0) -> dict:
    splits = jax.random.split(jax.random.key(seed), 7)
    pair = normal_values(splits[0], (N, N, C), 1.0, 6.0, ((0, 4), (1, 32)))
    norm_in = jnp.clip(1.0 + 0.18 * jax.random.normal(splits[1], (2, C), jnp.float32), 0.1, 1.9)
    proj_weight = normal_values(splits[2], (2, C, 4 * CH), C ** -0.5, 0.5)
    gate_weight = normal_values(splits[3], (2, C, C), C ** -0.5, 0.5)
    norm_out = jnp.clip(1.0 + 0.18 * jax.random.normal(splits[4], (2, CH), jnp.float32), 0.1, 1.9)
    out_weight = normal_values(splits[5], (2, CH, C), CH ** -0.5, 0.5)
    return dict(pair=pair, norm_in=norm_in, proj_weight=proj_weight, gate_weight=gate_weight, norm_out=norm_out, out_weight=out_weight)


def norm_rows(values, norm_gain):
    row_mean = lax.optimization_barrier(jnp.mean(values, -1, keepdims=True))
    centered = values - row_mean
    variance = lax.optimization_barrier(jnp.mean(centered * centered, -1, keepdims=True))
    return centered * lax.rsqrt(variance + 1e-05) * norm_gain

def triangle(pair_full, pass_index, norm_in, proj_weight, gate_weight, norm_out, out_weight):
    total = pair_full.shape[0]
    blocks = pair_full.reshape(16, total // 16, total, C)

    def project(block):
        normed = norm_rows(block.astype(jnp.float32), norm_in[pass_index]).astype(jnp.bfloat16).reshape(-1, C)
        projected = jnp.dot(normed, proj_weight[pass_index], preferred_element_type=jnp.float32)
        left_proj = jax.nn.sigmoid(projected[:, CH:2 * CH]) * projected[:, :CH]
        right_proj = jax.nn.sigmoid(projected[:, 3 * CH:]) * projected[:, 2 * CH:3 * CH]
        return jnp.stack([left_proj, right_proj]).astype(jnp.bfloat16)
    sides = lax.map(project, blocks)
    sides = sides.transpose(1, 0, 2, 3).reshape(2, total, total, CH).transpose(3, 0, 1, 2)

    def channel(pair_of):
        if pass_index == 0:
            contracted = jnp.dot(pair_of[0], pair_of[1].T, preferred_element_type=jnp.float32)
        else:
            contracted = jnp.dot(pair_of[0].T, pair_of[1], preferred_element_type=jnp.float32)
        return contracted.astype(jnp.bfloat16)
    mixed_vals = lax.map(channel, sides)
    mixed_blocks = mixed_vals.transpose(1, 2, 0).reshape(16, total // 16, total, CH)

    def finish(items):
        block, mixed_block = items
        block_f = block.astype(jnp.float32).reshape(-1, C)
        normed = norm_rows(block_f, norm_in[pass_index]).astype(jnp.bfloat16)
        gate_vals = jax.nn.sigmoid(jnp.dot(normed, gate_weight[pass_index], preferred_element_type=jnp.float32))
        normed_mix = norm_rows(mixed_block.reshape(-1, CH).astype(jnp.float32), norm_out[pass_index]).astype(jnp.bfloat16)
        projected_out = jnp.dot(normed_mix, out_weight[pass_index], preferred_element_type=jnp.float32)
        return (block_f + gate_vals * projected_out).astype(jnp.bfloat16).reshape(block.shape)
    return lax.map(finish, (blocks, mixed_blocks)).reshape(total, total, C)

def reference(pair, norm_in, proj_weight, gate_weight, norm_out, out_weight):
    current = pair
    for pass_index in range(2):
        current = triangle(current, pass_index, norm_in, proj_weight, gate_weight, norm_out, out_weight)
    return current
```

```python
import functools

import jax
import jax.numpy as jnp
from jax import lax
from jax.experimental import pallas as pl
from jax.experimental.pallas import tpu as pltpu
from jax.sharding import PartitionSpec as P

F32, BF16 = jnp.float32, jnp.bfloat16
MESH = pl.DeviceIdType.MESH

ROWS, COLS, C = 192, 24, 128
CHIPS = 64
PAIRS = 18
TOKENS = 768


def chip_coords():
    row, col = lax.axis_index("row"), lax.axis_index("col")
    return col // 8, (row // 2) * 2 + col % 2, (col // 2) % 4, row % 2


def peer(step, x, y, z):
    s = lax.rem(step * 37, CHIPS)
    px = lax.rem(x + s // 16, 4)
    py = lax.rem(y + lax.rem(s // 4, 4), 4)
    pz = lax.rem(z + lax.rem(s, 4), 4)
    return py // 2, px * 8 + pz * 2 + lax.rem(py, 2)


def norm_cols(values, gain):
    mean = jnp.mean(values, 0, keepdims=True)
    centered = values - mean
    variance = jnp.mean(centered * centered, 0, keepdims=True)
    return centered * lax.rsqrt(variance + 1e-05) * gain


def kernel(
    pair, norm_in, proj_w, gate_w, norm_out, out_w, out,
    zt, nb, gate, msg, left_right0, left_right1, xs, xr, part_out, part_in, part_own, ret, mix0, mix1, work,
    wfa, wfb, proj_a, gate_a, out_a, gain_in, gain_out, x2,
    fwd_send, fwd_recv, ret_send, ret_recv, core_send, core_recv,
):
    x, y, z, core = chip_coords()
    y_hi = y // 2
    col = lax.axis_index("col")
    me = y_hi * 32 + col
    sibling = (y_hi * 2 + 1 - core, col)

    def pick(a, b):
        return jnp.where(lax.broadcasted_iota(jnp.int32, a.shape, 1) < 64, a, b)

    barrier = pltpu.get_barrier_semaphore()
    pl.semaphore_signal(barrier, inc=1, device_id=sibling, device_id_type=MESH)

    @pl.loop(1, CHIPS)
    def _(step):
        py, pc = peer(step, x, y, z)
        pl.semaphore_signal(barrier, inc=1, device_id=(py * 2 + core, pc), device_id_type=MESH)

    for p in range(2):
        wt = proj_w[p].astype(F32).T
        wfa[...] = jnp.zeros_like(wfa)
        wfb[...] = jnp.zeros_like(wfb)
        wfa[pl.ds(0, 512, stride=2), :] = wt
        wfb[pl.ds(1, 512, stride=2), :] = wt
        proj_a[p, :, 0:128] = wfa[...].astype(BF16)
        proj_a[p, :, 128:256] = wfb[...].astype(BF16)
        gt = gate_w[p].astype(F32).T.astype(BF16)
        wfa[pl.ds(0, 64, stride=2), :] = out_w[p, 0:64].astype(F32)
        wfa[pl.ds(1, 64, stride=2), :] = out_w[p, 64:128].astype(F32)
        ot = wfa[0:128].T.astype(BF16)
        zero = jnp.zeros((128, 128), BF16)
        for dst, block in ((gate_a, gt), (out_a, ot)):
            dst[p, 0:128, 0:128] = block
            dst[p, 0:128, 128:256] = zero
            dst[p, 128:256, 0:128] = zero
            dst[p, 128:256, 128:256] = block
        picked = lax.broadcasted_iota(jnp.int32, (2, 128), 0) == p
        gain = jnp.sum(jnp.where(picked, norm_in[...], 0.0), 0, keepdims=True)
        gain_in[p] = jnp.broadcast_to(gain, (128, 128)).T
        gain = jnp.sum(jnp.where(picked, norm_out[...], 0.0), 0, keepdims=True)
        gain = jnp.broadcast_to(gain, (128, 128)).T
        wfa[pl.ds(0, 64, stride=2), :] = gain[0:64]
        wfa[pl.ds(1, 64, stride=2), :] = gain[64:128]
        gain_out[p] = wfa[0:128]

    work[...] = pair[...].astype(F32)

    @pl.loop(0, 12)
    def _(tp):
        for e in range(2):
            zt[tp, e * 128:(e + 1) * 128] = work[pl.ds(2 * tp + e, 128, stride=24), :].T.astype(BF16)

    @pl.loop(0, 6)
    def _(tp):
        for e in range(2):
            m = 2 * tp + e
            a = work[pl.ds(128 * 24 + m + 12 * y_hi, 64, stride=24), :]
            b = work[pl.ds(128 * 24 + m + 12 * (1 - y_hi), 64, stride=24), :]
            zt[12 + tp, e * 128:(e + 1) * 128] = jnp.concatenate([a, b], 0).T.astype(BF16)

    def project(p, u):
        for e in range(2):
            tp = 2 * u + e
            for h in range(2):
                rows = slice(h * 128, (h + 1) * 128)
                nb[tp, rows] = norm_cols(zt[tp, rows].astype(F32), gain_in[p]).astype(BF16)
        n = jnp.concatenate([nb[2 * u], nb[2 * u + 1]], 1)
        for side in range(2):
            a = proj_a[p, side * 512:(side + 1) * 512]
            got = jnp.dot(a, n, preferred_element_type=F32)
            val = (jax.nn.sigmoid(got[256:512]) * got[0:256]).astype(BF16)
            for ab in range(2):
                for e in range(2):
                    block = val[ab * 128:(ab + 1) * 128, e * 128:(e + 1) * 128]
                    msg[ab * 2 + side, 2 * u + e] = block.reshape(64, 2, 128)

    def gates(p):
        @pl.loop(0, 9)
        def _(u):
            n = jnp.concatenate([nb[2 * u], nb[2 * u + 1]], 1)
            g = jax.nn.sigmoid(jnp.dot(gate_a[p], n, preferred_element_type=F32))
            gate[2 * u] = g[:, 0:128]
            gate[2 * u + 1] = g[:, 128:256]

    def send_all(src_of, dst, send, recv):
        @pl.loop(1, CHIPS)
        def _(step):
            py, pc = peer(step, x, y, z)
            pltpu.make_async_remote_copy(
                src_ref=src_of(py * 32 + pc), dst_ref=dst, send_sem=send, recv_sem=recv,
                device_id=(py * 2 + core, pc), device_id_type=MESH,
            ).start()
        pltpu.make_async_copy(src_of(me), dst, recv).start()

    def wait_bytes(ref, sem):
        pltpu.make_async_copy(ref, ref, sem).wait()

    def build(src, i):
        t = src[i, 0:32, 12:18].reshape(384, 128).astype(F32)
        v = src[i, 32:64, 12:18].reshape(384, 128).astype(F32)
        xs[i, :, 0:128] = src[i, 0:32, 0:12].reshape(768, 128)
        xs[i, :, 128:256] = src[i, 32:64, 0:12].reshape(768, 128)
        x2[:, 0] = pick(t, v).astype(BF16).reshape(32, 6, 2, 128)
        x2[:, 1] = pltpu.roll(pick(v, t), 64, 1).astype(BF16).reshape(32, 6, 2, 128)
        xs[i, :, 256:384] = x2[...].reshape(768, 128)

    def core_copy(src, dst, i):
        return pltpu.make_async_remote_copy(
            src_ref=src, dst_ref=dst, send_sem=core_send.at[i], recv_sem=core_recv.at[i],
            device_id=sibling, device_id_type=MESH,
        )

    def mix_out():
        for ab in range(2):
            build(left_right0, ab * 2 + 1)
        copies = [core_copy(xs.at[ab * 2 + 1], xr.at[ab], ab) for ab in range(2)]
        for copy in copies:
            copy.start()
        for ab in range(2):
            build(left_right0, ab * 2)

        def contract(ab, right, owner):
            got = lax.dot_general(right, xs[ab * 2], (((0,), (0,)), ((), ())), preferred_element_type=F32)
            for it in range(3):
                at = it * 1536 + ab
                piece = got[:, it * 128:(it + 1) * 128]
                work[pl.ds(at + owner * 384, 128, stride=2), :] = piece[0:128]
                work[pl.ds(at + owner * 384 + 768, 128, stride=2), :] = piece[128:256]
                work[pl.ds(at + owner * 384 + 256, 64, stride=2), :] = piece[256:320]
                work[pl.ds(at + owner * 384 + 1024, 64, stride=2), :] = piece[320:384]

        for ab in range(2):
            contract(ab, xs[ab * 2 + 1], core)
        for ab in range(2):
            copies[ab].wait()
            contract(ab, xr[ab], 1 - core)

    def mix_in():
        for i in range(4):
            build(left_right1, i)

        def contract(ab, owner):
            first = pl.multiple_of(owner * 192, 64)
            i = ab * 2
            left = jnp.concatenate(
                [
                    xs[i, pl.ds(first, 128), :],
                    xs[i, pl.ds(first + 384, 128), :],
                    xs[i, pl.ds(first + 128, 64), :],
                    xs[i, pl.ds(first + 512, 64), :],
                ],
                0,
            )
            return lax.dot_general(xs[i + 1], left, (((1,), (1,)), ((), ())), preferred_element_type=F32)

        copies = []
        for ab in range(2):
            got = contract(ab, 1 - core)
            for it in range(3):
                part_out[ab, it] = got[:, it * 128:(it + 1) * 128].astype(BF16)
            copies.append(core_copy(part_out.at[ab], part_in.at[ab], 2 + ab))
            copies[ab].start()
        for ab in range(2):
            got = contract(ab, core)
            for it in range(3):
                part_own[ab, it] = got[:, it * 128:(it + 1) * 128]
        for ab in range(2):
            copies[ab].wait()
            for it in range(3):
                work[pl.ds(it * 1536 + ab, 768, stride=2), :] = part_own[ab, it] + part_in[ab, it].astype(F32)

    def pack():
        for it in range(2):
            rows = work[it * 1536:(it + 1) * 1536].astype(BF16)
            ret[it * 32:(it + 1) * 32, 0:24] = rows.reshape(32, 24, 2, 128)

        @pl.loop(0, 32)
        def _(q):
            first = pl.multiple_of(3072 + 48 * q, 8)
            top = work[pl.ds(first, 24), :]
            bot = pltpu.roll(work[pl.ds(first + 24, 24), :], 64, 1)
            ret[q, 24:36] = pick(top, bot).astype(BF16).reshape(12, 2, 128)
            ret[32 + q, 24:36] = pick(bot, top).astype(BF16).reshape(12, 2, 128)

    def finish(p, mix, u):
        cols = []
        for e in range(2):
            halves = []
            for h in range(2):
                vals = mix[2 * (2 * u + e) + h].reshape(128, 128).astype(F32)
                halves.append(norm_cols(vals, gain_out[p]).astype(BF16))
            cols.append(jnp.concatenate(halves, 0))
        got = jnp.dot(out_a[p], jnp.concatenate(cols, 1), preferred_element_type=F32)
        for e in range(2):
            tp = 2 * u + e
            zt[tp] = (zt[tp].astype(F32) + gate[tp] * got[:, e * 128:(e + 1) * 128]).astype(BF16)

    @pl.loop(0, 9)
    def _(u):
        project(0, u)

    pl.semaphore_wait(barrier, CHIPS)

    for p in range(2):
        arrived, mixed = ((left_right0, mix0), (left_right1, mix1))[p]
        send_all(lambda d: msg.at[:, :, d], arrived.at[:, me], fwd_send.at[p], fwd_recv.at[p])
        gates(p)
        wait_bytes(arrived, fwd_recv.at[p])
        (mix_out, mix_in)[p]()
        pack()
        send_all(lambda d: ret.at[d], mixed.at[:, me], ret_send.at[p], ret_recv.at[p])
        wait_bytes(msg.at[:, :, pl.ds(0, CHIPS - 1)], fwd_send.at[p])
        wait_bytes(mixed, ret_recv.at[p])
        wait_bytes(ret.at[pl.ds(0, CHIPS - 1)], ret_send.at[p])

        @pl.loop(0, 9)
        def _(u):
            finish(p, mixed, u)
            if p == 0:
                project(1, u)

    @pl.loop(0, 12)
    def _(tp):
        for e in range(2):
            work[pl.ds(2 * tp + e, 128, stride=24), :] = zt[tp, e * 128:(e + 1) * 128].astype(F32).T

    @pl.loop(0, 6)
    def _(tp):
        for e in range(2):
            m = 2 * tp + e
            vals = zt[12 + tp, e * 128:(e + 1) * 128].astype(F32).T
            work[pl.ds(128 * 24 + m + 12 * y_hi, 64, stride=24), :] = vals[0:64]
            work[pl.ds(128 * 24 + m + 12 * (1 - y_hi), 64, stride=24), :] = vals[64:128]

    out[...] = work[...].astype(BF16)


def on_device(pair, norm_in, proj_weight, gate_weight, norm_out, out_weight):
    vmem = pl.BlockSpec(memory_space=pltpu.VMEM)
    updated = pl.pallas_call(
        kernel,
        out_shape=jax.ShapeDtypeStruct((ROWS * COLS, C), BF16),
        in_specs=[vmem] * 6,
        out_specs=vmem,
        scratch_shapes=[
            pltpu.VMEM((PAIRS, 256, 128), BF16),
            pltpu.VMEM((PAIRS, 256, 128), BF16),
            pltpu.VMEM((PAIRS, 256, 128), F32),
            pltpu.VMEM((4, PAIRS, CHIPS, 2, 128), BF16),
            pltpu.VMEM((4, CHIPS, PAIRS, 2, 128), BF16),
            pltpu.VMEM((4, CHIPS, PAIRS, 2, 128), BF16),
            pltpu.VMEM((4, TOKENS, 384), BF16),
            pltpu.VMEM((2, TOKENS, 384), BF16),
            pltpu.VMEM((2, 3, TOKENS, 128), BF16),
            pltpu.VMEM((2, 3, TOKENS, 128), BF16),
            pltpu.VMEM((2, 3, TOKENS, 128), F32),
            pltpu.VMEM((CHIPS, 36, 2, 128), BF16),
            pltpu.VMEM((36, CHIPS, 2, 128), BF16),
            pltpu.VMEM((36, CHIPS, 2, 128), BF16),
            pltpu.VMEM((ROWS * COLS, 128), F32),
            pltpu.VMEM((1024, 128), F32),
            pltpu.VMEM((1024, 128), F32),
            pltpu.VMEM((2, 1024, 256), BF16),
            pltpu.VMEM((2, 256, 256), BF16),
            pltpu.VMEM((2, 256, 256), BF16),
            pltpu.VMEM((2, 128, 128), F32),
            pltpu.VMEM((2, 128, 128), F32),
            pltpu.VMEM((32, 2, 6, 2, 128), BF16),
        ] + [pltpu.SemaphoreType.DMA((2,))] * 4 + [pltpu.SemaphoreType.DMA((4,))] * 2,
        compiler_params=pltpu.CompilerParams(
            collective_id=0, has_side_effects=True, vmem_limit_bytes=56 * 2**20
        ),
    )(pair.reshape(ROWS * COLS, C), norm_in, proj_weight, gate_weight, norm_out, out_weight)
    return updated.reshape(ROWS, COLS, C)


def solution(mesh):
    placed = (P("row", "col", None), P(), P(), P(), P(), P())
    return jax.shard_map(
        on_device, mesh=mesh, in_specs=placed, out_specs=P("row", "col", None), check_vma=False
    )
```

```python
import functools

import jax
import jax.numpy as jnp
from jax import lax
from jax.experimental import pallas as pl
from jax.experimental.pallas import tpu as pltpu
from jax.sharding import PartitionSpec as P

F32, BF16 = jnp.float32, jnp.bfloat16
MESH = pl.DeviceIdType.MESH

ROWS, COLS, C = 192, 24, 128
CHIPS = 64
PAIRS = 18
TOKENS = 768


def chip_coords():
    row, col = lax.axis_index("row"), lax.axis_index("col")
    return col // 8, (row // 2) * 2 + col % 2, (col // 2) % 4, row % 2


def norm_cols(values, gain):
    mean = jnp.mean(values, 0, keepdims=True)
    centered = values - mean
    variance = jnp.mean(centered * centered, 0, keepdims=True)
    return centered * lax.rsqrt(variance + 1e-05) * gain


def sigmoid(values):
    return 0.5 * jnp.tanh(0.5 * values) + 0.5


def kernel(
    pair, norm_in, proj_w, gate_w, norm_out, out_w, out,
    pbuf, zt, nb, gate, msg, left_right0, left_right1, xl0, xt0, xt0_far, xl1, xr1, xl1_far, xr1_far, acc, ret, mix0, mix1,
    work, wfa, wfb, proj_a, gate_a, out_a, gain_in, gain_out, x2,
    fwd_send, fwd_recv, ret_send, ret_recv, core_send, core_recv, local,
):
    x, y, z, core = chip_coords()
    y_hi = y // 2
    col = lax.axis_index("col")
    me = y_hi * 32 + col
    sibling = (y_hi * 2 + 1 - core, col)
    y_of = [lax.rem(y + b, 4) for b in range(4)]
    row_of = [v // 2 for v in y_of]
    low_of = [lax.rem(v, 2) for v in y_of]
    z_of = [lax.rem(z + c, 4) * 2 for c in range(4)]

    def pick(a, b):
        return jnp.where(lax.broadcasted_iota(jnp.int32, a.shape, 1) < 64, a, b)

    def each_peer(act):
        @pl.loop(0, 4)
        def _(i):
            for n in range(16):
                b, c = n % 4, (n // 4 + n) % 4
                px = lax.rem(x + (b + c) % 4 + i, 4) * 8

                def one():
                    act(row_of[b], px + low_of[b] + z_of[c])

                if n == 0:
                    pl.when(i > 0)(one)
                else:
                    one()

    def send_all(src_of, dst, send, recv):
        def one(py, pc):
            pltpu.make_async_remote_copy(
                src_ref=src_of(py * 32 + pc), dst_ref=dst, send_sem=send, recv_sem=recv,
                device_id=(py * 2 + core, pc), device_id_type=MESH,
            ).start()

        each_peer(one)
        pltpu.make_async_copy(src_of(me), dst, recv).start()

    def wait_bytes(ref, sem):
        pltpu.make_async_copy(ref, ref, sem).wait()

    loads = [
        pltpu.make_async_copy(pair.at[pl.ds(a, n)], pbuf.at[pl.ds(a, n)], local.at[i])
        for i, (a, n) in enumerate(((0, 3072), (3072, 1536)))
    ]
    for load in loads:
        load.start()

    barrier = pltpu.get_barrier_semaphore()
    pl.semaphore_signal(barrier, inc=1, device_id=sibling, device_id_type=MESH)
    each_peer(lambda py, pc: pl.semaphore_signal(
        barrier, inc=1, device_id=(py * 2 + core, pc), device_id_type=MESH))

    def picked_gain(ref, p):
        rows = lax.broadcasted_iota(jnp.int32, (2, 128), 0) == p
        row = jnp.sum(jnp.where(rows, ref[...], 0.0), 0, keepdims=True)
        return jnp.broadcast_to(row, (128, 128)).T

    def prepare_in(p):
        wt = proj_w[p].astype(F32).T
        wfa[pl.ds(0, 512, stride=2), :] = wt
        wfa[pl.ds(1, 512, stride=2), :] = jnp.zeros_like(wt)
        wfb[pl.ds(0, 512, stride=2), :] = jnp.zeros_like(wt)
        wfb[pl.ds(1, 512, stride=2), :] = wt
        proj_a[p, :, 0:128] = wfa[...].astype(BF16)
        proj_a[p, :, 128:256] = wfb[...].astype(BF16)
        gain_in[p] = picked_gain(norm_in, p)

    def prepare_out(p):
        gt = gate_w[p].astype(F32).T.astype(BF16)
        wfa[pl.ds(0, 64, stride=2), :] = out_w[p, 0:64].astype(F32)
        wfa[pl.ds(1, 64, stride=2), :] = out_w[p, 64:128].astype(F32)
        ot = wfa[0:128].T.astype(BF16)
        zero = jnp.zeros((128, 128), BF16)
        for dst, block in ((gate_a, gt), (out_a, ot)):
            dst[p, 0:128, 0:128] = block
            dst[p, 0:128, 128:256] = zero
            dst[p, 128:256, 0:128] = zero
            dst[p, 128:256, 128:256] = block
        gain = picked_gain(norm_out, p)
        wfa[pl.ds(0, 64, stride=2), :] = gain[0:64]
        wfa[pl.ds(1, 64, stride=2), :] = gain[64:128]
        gain_out[p] = wfa[0:128]

    def half_rows(m, first):
        return pl.ds(128 * 24 + m + 12 * first, 64, stride=24)

    def load_tiles(tp, mixed):
        for e in range(2):
            if mixed:
                m = 2 * tp + e - 24
                vals = jnp.concatenate([work[half_rows(m, y_hi), :], work[half_rows(m, 1 - y_hi), :]], 0)
            else:
                vals = work[pl.ds(2 * tp + e, 128, stride=24), :]
            zt[tp, e * 128:(e + 1) * 128] = vals.T.astype(BF16)

    def store_tiles(tp, mixed):
        for e in range(2):
            vals = zt[tp, e * 128:(e + 1) * 128].astype(F32).T
            if mixed:
                m = 2 * tp + e - 24
                work[half_rows(m, y_hi), :] = vals[0:64]
                work[half_rows(m, 1 - y_hi), :] = vals[64:128]
            else:
                work[pl.ds(2 * tp + e, 128, stride=24), :] = vals

    def project(p, u):
        for e in range(2):
            tp = 2 * u + e
            for h in range(2):
                rows = slice(h * 128, (h + 1) * 128)
                nb[tp, rows] = norm_cols(zt[tp, rows].astype(F32), gain_in[p]).astype(BF16)
        n = jnp.concatenate([nb[2 * u], nb[2 * u + 1]], 1)
        for side in range(2):
            a = proj_a[p, side * 512:(side + 1) * 512]
            got = jnp.dot(a, n, preferred_element_type=F32)
            val = (sigmoid(got[256:512]) * got[0:256]).astype(BF16)
            for ab in range(2):
                for e in range(2):
                    block = val[ab * 128:(ab + 1) * 128, e * 128:(e + 1) * 128]
                    msg[ab * 2 + side, 2 * u + e] = block.reshape(64, 2, 128)

    def gates(p):
        @pl.loop(0, 9)
        def _(u):
            n = jnp.concatenate([nb[2 * u], nb[2 * u + 1]], 1)
            g = sigmoid(jnp.dot(gate_a[p], n, preferred_element_type=F32))
            gate[2 * u] = g[:, 0:128]
            gate[2 * u + 1] = g[:, 128:256]

    def send_group(p, g):
        arrived = (left_right0, left_right1)[p]
        send_all(
            lambda d: msg.at[:, pl.ds(6 * g, 6), d], arrived.at[:, me, pl.ds(6 * g, 6)],
            fwd_send.at[p, g], fwd_recv.at[p, g],
        )

    def wait_group(p, g):
        arrived = (left_right0, left_right1)[p]
        wait_bytes(arrived.at[:, :, pl.ds(6 * g, 6)], fwd_recv.at[p, g])

    def wait_group_sent(p, g):
        wait_bytes(msg.at[:, pl.ds(6 * g, 6), pl.ds(0, CHIPS - 1)], fwd_send.at[p, g])

    def main_cols(src, i, it):
        return src[i, 32 * it:32 * (it + 1), 0:12].reshape(768, 128)

    def mixed_cols(src, i):
        t = src[i, 0:32, 12:18].reshape(384, 128).astype(F32)
        v = src[i, 32:64, 12:18].reshape(384, 128).astype(F32)
        x2[:, 0] = pick(t, v).astype(BF16).reshape(32, 6, 2, 128)
        x2[:, 1] = pltpu.roll(pick(v, t), 64, 1).astype(BF16).reshape(32, 6, 2, 128)
        return x2[...].reshape(768, 128)

    def core_copy(src, dst, i):
        return pltpu.make_async_remote_copy(
            src_ref=src, dst_ref=dst, send_sem=core_send.at[i], recv_sem=core_recv.at[i],
            device_id=sibling, device_id_type=MESH,
        )

    def place(ab, got, first_it, jt, owner):
        for n in range(got.shape[1] // 128):
            at = (first_it + n) * 1536 + ab + owner * 384
            piece = got[:, n * 128:(n + 1) * 128]
            if jt < 2:
                work[pl.ds(at + 768 * jt, 128, stride=2), :] = piece
            else:
                work[pl.ds(at + 256, 64, stride=2), :] = piece[0:64]
                work[pl.ds(at + 1024, 64, stride=2), :] = piece[64:128]

    def mix_out():
        src = left_right0
        wait_group(0, 0)
        wait_group(0, 1)
        for ab in range(2):
            for it in range(2):
                xt0[ab, it * 128:(it + 1) * 128] = main_cols(src, ab * 2 + 1, it).T
        main = core_copy(xt0.at[:, pl.ds(0, 256)], xt0_far.at[:, pl.ds(0, 256)], 0)
        main.start()
        for ab in range(2):
            for it in range(2):
                xl0[ab, :, it * 128:(it + 1) * 128] = main_cols(src, ab * 2, it)

        def contract(right, jt, cols, owner):
            for ab in range(2):
                r = right[ab, jt * 128:(jt + 1) * 128]
                got = jnp.dot(r, xl0[ab, :, cols], preferred_element_type=F32)
                place(ab, got, cols.start // 128, jt, owner)

        for jt in range(2):
            contract(xt0, jt, slice(0, 256), core)
        main.wait()
        for jt in range(2):
            contract(xt0_far, jt, slice(0, 256), 1 - core)

        wait_group(0, 2)
        for ab in range(2):
            xt0[ab, 256:384] = mixed_cols(src, ab * 2 + 1).T
        mixed = core_copy(xt0.at[:, pl.ds(256, 128)], xt0_far.at[:, pl.ds(256, 128)], 1)
        mixed.start()
        for ab in range(2):
            xl0[ab, :, 256:384] = mixed_cols(src, ab * 2)
        contract(xt0, 2, slice(0, 384), core)
        for jt in range(2):
            contract(xt0, jt, slice(256, 384), core)
            contract(xt0_far, jt, slice(256, 384), 1 - core)
        mixed.wait()
        contract(xt0_far, 2, slice(0, 384), 1 - core)

    def own_rows(ref):
        return jnp.concatenate([ref[0, 0:128], ref[1, 0:128], ref[0, 128:192], ref[1, 128:192]], 0)

    def mix_in():
        src = left_right1

        def exchange(cols, i):
            right = core_copy(xr1.at[:, :, cols], xr1_far.at[:, :, cols], i)
            left = core_copy(xl1.at[:, :, 1 - core, :, cols], xl1_far.at[:, :, :, cols], i + 1)
            right.start()
            left.start()
            return right, left

        def contract(ab, cols):
            right = jnp.concatenate([xr1[ab, :, cols], xr1_far[ab, :, cols]], 1)
            own = own_rows(xl1.at[ab, :, core, :, cols])
            far = own_rows(xl1_far.at[ab, :, :, cols])
            left = jnp.concatenate([own, far], 1)
            return lax.dot_general(right, left, (((1,), (1,)), ((), ())), preferred_element_type=F32)

        wait_group(1, 0)
        wait_group(1, 1)
        for ab in range(2):
            for it in range(2):
                xr1[ab, :, it * 128:(it + 1) * 128] = main_cols(src, ab * 2 + 1, it)
                xl1[ab, :, :, :, it * 128:(it + 1) * 128] = main_cols(src, ab * 2, it).reshape(2, 2, 192, 128)
        copies = exchange(pl.ds(0, 256), 2)
        for copy in copies:
            copy.wait()
        for ab in range(2):
            acc[ab] = contract(ab, pl.ds(0, 256))

        wait_group(1, 2)
        for ab in range(2):
            xr1[ab, :, 256:384] = mixed_cols(src, ab * 2 + 1)
            xl1[ab, :, :, :, 256:384] = mixed_cols(src, ab * 2).reshape(2, 2, 192, 128)
        copies = exchange(pl.ds(256, 128), 4)
        for copy in copies:
            copy.wait()
        for ab in range(2):
            got = contract(ab, pl.ds(256, 128)) + acc[ab]
            for it in range(3):
                work[pl.ds(it * 1536 + ab, 768, stride=2), :] = got[:, it * 128:(it + 1) * 128]

    def give_back(p):
        mixed = (mix0, mix1)[p]
        for it in range(2):
            rows = work[it * 1536:(it + 1) * 1536].astype(BF16)
            ret[it * 32:(it + 1) * 32, 0:24] = rows.reshape(32, 24, 2, 128)
        send_all(lambda d: ret.at[d, pl.ds(0, 24)], mixed.at[pl.ds(0, 24), me], ret_send.at[p, 0], ret_recv.at[p, 0])

        @pl.loop(0, 32)
        def _(q):
            first = pl.multiple_of(3072 + 48 * q, 8)
            top = work[pl.ds(first, 24), :]
            bot = pltpu.roll(work[pl.ds(first + 24, 24), :], 64, 1)
            ret[q, 24:36] = pick(top, bot).astype(BF16).reshape(12, 2, 128)
            ret[32 + q, 24:36] = pick(bot, top).astype(BF16).reshape(12, 2, 128)

        send_all(lambda d: ret.at[d, pl.ds(24, 12)], mixed.at[pl.ds(24, 12), me], ret_send.at[p, 1], ret_recv.at[p, 1])

    def wait_back(p, part):
        rows = ((0, 24), (24, 12))[part]
        wait_bytes((mix0, mix1)[p].at[pl.ds(*rows)], ret_recv.at[p, part])

    def wait_back_sent(p):
        for part, rows in enumerate(((0, 24), (24, 12))):
            wait_bytes(ret.at[pl.ds(0, CHIPS - 1), pl.ds(*rows)], ret_send.at[p, part])

    def finish(p, u):
        mix = (mix0, mix1)[p]
        cols = []
        for e in range(2):
            halves = []
            for h in range(2):
                vals = mix[2 * (2 * u + e) + h].reshape(128, 128).astype(F32)
                halves.append(norm_cols(vals, gain_out[p]).astype(BF16))
            cols.append(jnp.concatenate(halves, 0))
        got = jnp.dot(out_a[p], jnp.concatenate(cols, 1), preferred_element_type=F32)
        for e in range(2):
            tp = 2 * u + e
            zt[tp] = (zt[tp].astype(F32) + gate[tp] * got[:, e * 128:(e + 1) * 128]).astype(BF16)

    prepare_in(0)
    for g in range(3):
        if g == 0:
            loads[0].wait()
            work[0:3072] = pbuf[0:3072].astype(F32)
        if g == 2:
            loads[1].wait()
            work[3072:4608] = pbuf[3072:4608].astype(F32)

        @pl.loop(3 * g, 3 * g + 3)
        def _(u):
            for e in range(2):
                load_tiles(2 * u + e, g == 2)
            project(0, u)

        if g == 0:
            pl.semaphore_wait(barrier, CHIPS)
        send_group(0, g)

    prepare_out(0)
    gates(0)
    prepare_in(1)
    prepare_out(1)
    mix_out()
    give_back(0)
    for g in range(3):
        wait_group_sent(0, g)
    for g in range(3):
        if g != 1:
            wait_back(0, g // 2)

        @pl.loop(3 * g, 3 * g + 3)
        def _(u):
            finish(0, u)
            project(1, u)

        send_group(1, g)

    gates(1)
    wait_back_sent(0)
    mix_in()
    give_back(1)
    for g in range(3):
        wait_group_sent(1, g)
    stores = [
        pltpu.make_async_copy(pbuf.at[pl.ds(a, n)], out.at[pl.ds(a, n)], local.at[2 + i])
        for i, (a, n) in enumerate(((0, 3072), (3072, 1536)))
    ]
    for part, (first, last) in enumerate(((0, 6), (6, 9))):
        wait_back(1, part)

        @pl.loop(first, last)
        def _(u):
            finish(1, u)
            for e in range(2):
                store_tiles(2 * u + e, part == 1)

        rows = ((0, 3072), (3072, 4608))[part]
        pbuf[rows[0]:rows[1]] = work[rows[0]:rows[1]].astype(BF16)
        stores[part].start()
    wait_back_sent(1)
    for store in stores:
        store.wait()


def on_device(pair, norm_in, proj_weight, gate_weight, norm_out, out_weight):
    vmem = pl.BlockSpec(memory_space=pltpu.VMEM)
    hbm = pl.BlockSpec(memory_space=pl.ANY)
    updated = pl.pallas_call(
        kernel,
        out_shape=jax.ShapeDtypeStruct((ROWS * COLS, C), BF16),
        in_specs=[hbm] + [vmem] * 5,
        out_specs=hbm,
        scratch_shapes=[
            pltpu.VMEM((ROWS * COLS, C), BF16),
            pltpu.VMEM((PAIRS, 256, 128), BF16),
            pltpu.VMEM((PAIRS, 256, 128), BF16),
            pltpu.VMEM((PAIRS, 256, 128), F32),
            pltpu.VMEM((4, PAIRS, CHIPS, 2, 128), BF16),
            pltpu.VMEM((4, CHIPS, PAIRS, 2, 128), BF16),
            pltpu.VMEM((4, CHIPS, PAIRS, 2, 128), BF16),
            pltpu.VMEM((2, TOKENS, 384), BF16),
            pltpu.VMEM((2, 384, TOKENS), BF16),
            pltpu.VMEM((2, 384, TOKENS), BF16),
            pltpu.VMEM((2, 2, 2, 192, 384), BF16),
            pltpu.VMEM((2, TOKENS, 384), BF16),
            pltpu.VMEM((2, 2, 192, 384), BF16),
            pltpu.VMEM((2, TOKENS, 384), BF16),
            pltpu.VMEM((2, TOKENS, 384), F32),
            pltpu.VMEM((CHIPS, 36, 2, 128), BF16),
            pltpu.VMEM((36, CHIPS, 2, 128), BF16),
            pltpu.VMEM((36, CHIPS, 2, 128), BF16),
            pltpu.VMEM((ROWS * COLS, 128), F32),
            pltpu.VMEM((1024, 128), F32),
            pltpu.VMEM((1024, 128), F32),
            pltpu.VMEM((2, 1024, 256), BF16),
            pltpu.VMEM((2, 256, 256), BF16),
            pltpu.VMEM((2, 256, 256), BF16),
            pltpu.VMEM((2, 128, 128), F32),
            pltpu.VMEM((2, 128, 128), F32),
            pltpu.VMEM((32, 2, 6, 2, 128), BF16),
            pltpu.SemaphoreType.DMA((2, 3)),
            pltpu.SemaphoreType.DMA((2, 3)),
            pltpu.SemaphoreType.DMA((2, 2)),
            pltpu.SemaphoreType.DMA((2, 2)),
            pltpu.SemaphoreType.DMA((6,)),
            pltpu.SemaphoreType.DMA((6,)),
            pltpu.SemaphoreType.DMA((4,)),
        ],
        compiler_params=pltpu.CompilerParams(
            collective_id=0, has_side_effects=True, vmem_limit_bytes=56 * 2**20
        ),
    )(pair.reshape(ROWS * COLS, C), norm_in, proj_weight, gate_weight, norm_out, out_weight)
    return updated.reshape(ROWS, COLS, C)


def solution(mesh):
    placed = (P("row", "col", None), P(), P(), P(), P(), P())
    return jax.shard_map(
        on_device, mesh=mesh, in_specs=placed, out_specs=P("row", "col", None), check_vma=False
    )
```

```python
import functools

import jax
import jax.numpy as jnp
from jax import lax
from jax.experimental import pallas as pl
from jax.experimental.pallas import tpu as pltpu
from jax.sharding import PartitionSpec as P

F32, BF16 = jnp.float32, jnp.bfloat16
MESH = pl.DeviceIdType.MESH

ROWS, COLS, C = 192, 24, 128
CHIPS = 64
PAIRS = 18
THIRDS = ((0, 6), (6, 6), (12, 6))
FWD = ((((0, 18),), ((0, 18),)), (THIRDS, ((0, 18),)))
RET = ((((0, 18),), THIRDS), (((0, 18),), THIRDS))
TOKENS = 768


def chip_coords():
    row, col = lax.axis_index("row"), lax.axis_index("col")
    return col // 8, (row // 2) * 2 + col % 2, (col // 2) % 4, row % 2


def norm_cols(values, gain):
    mean = jnp.mean(values, 0, keepdims=True)
    centered = values - mean
    variance = jnp.mean(centered * centered, 0, keepdims=True)
    return centered * lax.rsqrt(variance + 1e-05) * gain


def sigmoid(values):
    return 0.5 * jnp.tanh(0.5 * values) + 0.5


def kernel(
    pair, norm_in, proj_w, gate_w, norm_out, out_w, out,
    pbuf, zt, nb, gate, msg, left_right0, left_right1, xl0, xt0, xt0_far, xl1, xr1, xl1_far, xr1_far, mixed, ret, mix0, mix1,
    work, wfa, wfb, proj_a, gate_a, out_a, gain_in, gain_out, x2,
    fwd_send, fwd_recv, ret_send, ret_recv, core_send, core_recv, local,
):
    x, y, z, core = chip_coords()
    y_hi = y // 2
    col = lax.axis_index("col")
    me = y_hi * 32 + col
    sibling = (y_hi * 2 + 1 - core, col)
    y_of = [lax.rem(y + b, 4) for b in range(4)]
    row_of = [v // 2 for v in y_of]
    low_of = [lax.rem(v, 2) for v in y_of]
    z_of = [lax.rem(z + c, 4) * 2 for c in range(4)]

    def pick(a, b):
        return jnp.where(lax.broadcasted_iota(jnp.int32, a.shape, 1) < 64, a, b)

    def each_peer(act):
        @pl.loop(0, 4)
        def _(i):
            for n in range(16):
                b, c = n % 4, (n // 4 + n) % 4
                px = lax.rem(x + (b + c) % 4 + i, 4) * 8

                def one():
                    act(row_of[b], px + low_of[b] + z_of[c])

                if n == 0:
                    pl.when(i > 0)(one)
                else:
                    one()

    def send_all(src_of, dst, send, recv):
        def one(py, pc):
            pltpu.make_async_remote_copy(
                src_ref=src_of(py * 32 + pc), dst_ref=dst, send_sem=send, recv_sem=recv,
                device_id=(py * 2 + core, pc), device_id_type=MESH,
            ).start()

        each_peer(one)
        pltpu.make_async_copy(src_of(me), dst, recv).start()

    def wait_bytes(ref, sem):
        pltpu.make_async_copy(ref, ref, sem).wait()

    loads = [
        pltpu.make_async_copy(pair.at[pl.ds(a, n)], pbuf.at[pl.ds(a, n)], local.at[i])
        for i, (a, n) in enumerate(((0, 3072), (3072, 1536)))
    ]
    for load in loads:
        load.start()

    barrier = pltpu.get_barrier_semaphore()
    pl.semaphore_signal(barrier, inc=1, device_id=sibling, device_id_type=MESH)
    each_peer(lambda py, pc: pl.semaphore_signal(
        barrier, inc=1, device_id=(py * 2 + core, pc), device_id_type=MESH))

    def picked_gain(ref, p):
        rows = lax.broadcasted_iota(jnp.int32, (2, 128), 0) == p
        row = jnp.sum(jnp.where(rows, ref[...], 0.0), 0, keepdims=True)
        return jnp.broadcast_to(row, (128, 128)).T

    def prepare_in(p):
        wt = proj_w[p].astype(F32).T
        wfa[pl.ds(0, 512, stride=2), :] = wt
        wfa[pl.ds(1, 512, stride=2), :] = jnp.zeros_like(wt)
        wfb[pl.ds(0, 512, stride=2), :] = jnp.zeros_like(wt)
        wfb[pl.ds(1, 512, stride=2), :] = wt
        proj_a[p, :, 0:128] = wfa[...].astype(BF16)
        proj_a[p, :, 128:256] = wfb[...].astype(BF16)
        gain_in[p] = picked_gain(norm_in, p)

    def prepare_out(p):
        gt = gate_w[p].astype(F32).T.astype(BF16)
        zero = jnp.zeros((128, 128), BF16)
        gate_a[p, 0:128, 0:128] = gt
        gate_a[p, 0:128, 128:256] = zero
        gate_a[p, 128:256, 0:128] = zero
        gate_a[p, 128:256, 128:256] = gt
        ow = out_w[p].astype(F32)
        for e in range(2):
            wfa[pl.ds(e, 128, stride=2), :] = ow
            wfa[pl.ds(1 - e, 128, stride=2), :] = jnp.zeros_like(ow)
            out_a[p, e * 128:(e + 1) * 128] = wfa[0:256].T.astype(BF16)
        gain = picked_gain(norm_out, p)
        for e in range(2):
            wfa[pl.ds(e, 128, stride=2), :] = gain
        gain_out[p] = wfa[0:256]

    def half_rows(m, first):
        return pl.ds(128 * 24 + m + 12 * first, 64, stride=24)

    def load_tiles(tp, mixed):
        for e in range(2):
            if mixed:
                m = 2 * tp + e - 24
                vals = jnp.concatenate([work[half_rows(m, y_hi), :], work[half_rows(m, 1 - y_hi), :]], 0)
            else:
                vals = work[pl.ds(2 * tp + e, 128, stride=24), :]
            zt[tp, e * 128:(e + 1) * 128] = vals.T.astype(BF16)

    def store_tiles(tp, mixed):
        for e in range(2):
            vals = zt[tp, e * 128:(e + 1) * 128].astype(F32).T
            if mixed:
                m = 2 * tp + e - 24
                work[half_rows(m, y_hi), :] = vals[0:64]
                work[half_rows(m, 1 - y_hi), :] = vals[64:128]
            else:
                work[pl.ds(2 * tp + e, 128, stride=24), :] = vals

    def project(p, u):
        for e in range(2):
            tp = 2 * u + e
            for h in range(2):
                rows = slice(h * 128, (h + 1) * 128)
                nb[tp, rows] = norm_cols(zt[tp, rows].astype(F32), gain_in[p]).astype(BF16)
        n = jnp.concatenate([nb[2 * u], nb[2 * u + 1]], 1)
        for side in range(2):
            a = proj_a[p, side * 512:(side + 1) * 512]
            got = jnp.dot(a, n, preferred_element_type=F32)
            val = (sigmoid(got[256:512]) * got[0:256]).astype(BF16)
            for ab in range(2):
                for e in range(2):
                    block = val[ab * 128:(ab + 1) * 128, e * 128:(e + 1) * 128]
                    msg[ab * 2 + side, 2 * u + e] = block.reshape(64, 2, 128)

    def gates(p):
        @pl.loop(0, 9)
        def _(u):
            n = jnp.concatenate([nb[2 * u], nb[2 * u + 1]], 1)
            g = sigmoid(jnp.dot(gate_a[p], n, preferred_element_type=F32))
            gate[2 * u] = g[:, 0:128]
            gate[2 * u + 1] = g[:, 128:256]

    def span(p, ab, n):
        return pl.ds(*FWD[p][ab][n])

    def send_group(p, ab, n):
        arrived = (left_right0, left_right1)[p]
        both = pl.ds(2 * ab, 2)
        send_all(
            lambda d: msg.at[both, span(p, ab, n), d], arrived.at[both, me, span(p, ab, n)],
            fwd_send.at[p, ab, n], fwd_recv.at[p, ab, n],
        )

    def wait_channel(p, ab):
        arrived = (left_right0, left_right1)[p]
        for n in range(len(FWD[p][ab])):
            wait_bytes(arrived.at[pl.ds(2 * ab, 2), :, span(p, ab, n)], fwd_recv.at[p, ab, n])

    def wait_sent(p):
        for ab in range(2):
            for n in range(len(FWD[p][ab])):
                wait_bytes(
                    msg.at[pl.ds(2 * ab, 2), span(p, ab, n), pl.ds(0, CHIPS - 1)], fwd_send.at[p, ab, n])

    def main_cols(src, i, it):
        return src[i, 32 * it:32 * (it + 1), 0:12].reshape(768, 128)

    def mixed_cols(src, i):
        t = src[i, 0:32, 12:18].reshape(384, 128).astype(F32)
        v = src[i, 32:64, 12:18].reshape(384, 128).astype(F32)
        x2[:, 0] = pick(t, v).astype(BF16).reshape(32, 6, 2, 128)
        x2[:, 1] = pltpu.roll(pick(v, t), 64, 1).astype(BF16).reshape(32, 6, 2, 128)
        return x2[...].reshape(768, 128)

    def core_copy(src, dst, i):
        return pltpu.make_async_remote_copy(
            src_ref=src, dst_ref=dst, send_sem=core_send.at[i], recv_sem=core_recv.at[i],
            device_id=sibling, device_id_type=MESH,
        )

    def mix_out(ab):
        src = left_right0
        wait_channel(0, ab)
        for it in range(2):
            xt0[ab, it * 128:(it + 1) * 128] = main_cols(src, ab * 2 + 1, it).T
        xt0[ab, 256:384] = mixed_cols(src, ab * 2 + 1).T
        copy = core_copy(xt0.at[ab], xt0_far.at[ab], ab)
        copy.start()
        for it in range(2):
            xl0[ab, :, it * 128:(it + 1) * 128] = main_cols(src, ab * 2, it)
        xl0[ab, :, 256:384] = mixed_cols(src, ab * 2)

        def contract(right, owner):
            got = jnp.dot(right, xl0[ab], preferred_element_type=F32)
            first = pl.multiple_of(owner * 192, 64)
            for it in range(3):
                piece = got[:, it * 128:(it + 1) * 128].astype(BF16)
                mixed[it, pl.ds(first, 128), :] = piece[0:128]
                mixed[it, pl.ds(first + 384, 128), :] = piece[128:256]
                mixed[it, pl.ds(first + 128, 64), :] = piece[256:320]
                mixed[it, pl.ds(first + 512, 64), :] = piece[320:384]

        contract(xt0[ab], core)
        copy.wait()
        contract(xt0_far[ab], 1 - core)

    def own_rows(ref):
        return jnp.concatenate([ref[0, 0:128], ref[1, 0:128], ref[0, 128:192], ref[1, 128:192]], 0)

    def mix_in(ab):
        src = left_right1
        wait_channel(1, ab)
        for it in range(2):
            xr1[ab, :, it * 128:(it + 1) * 128] = main_cols(src, ab * 2 + 1, it)
        xr1[ab, :, 256:384] = mixed_cols(src, ab * 2 + 1)
        right = core_copy(xr1.at[ab], xr1_far.at[ab], 2 + ab)
        right.start()
        for it in range(2):
            xl1[ab, :, :, :, it * 128:(it + 1) * 128] = main_cols(src, ab * 2, it).reshape(2, 2, 192, 128)
        xl1[ab, :, :, :, 256:384] = mixed_cols(src, ab * 2).reshape(2, 2, 192, 128)
        left = core_copy(xl1.at[ab, :, 1 - core], xl1_far.at[ab], 4 + ab)
        left.start()

        def contract(right, left):
            return lax.dot_general(right, left, (((1,), (1,)), ((), ())), preferred_element_type=F32)

        got = contract(xr1[ab], own_rows(xl1.at[ab, :, core]))
        right.wait()
        left.wait()
        got = got + contract(xr1_far[ab], own_rows(xl1_far.at[ab]))
        for it in range(3):
            mixed[it] = got[:, it * 128:(it + 1) * 128].astype(BF16)

    def send_back(p, ab, n):
        some = pl.ds(*RET[p][ab][n])
        send_all(
            lambda d: ret.at[ab, d, some], (mix0, mix1)[p].at[ab, some, me],
            ret_send.at[p, ab, n], ret_recv.at[p, ab, n],
        )

    def give_back(p, ab):
        for it in range(2):
            ret[ab, it * 32:(it + 1) * 32, 0:12] = mixed[it].reshape(32, 12, 2, 128)
        if ab == 1:
            send_back(p, ab, 0)
            send_back(p, ab, 1)
        x2[...] = mixed[2].reshape(32, 2, 6, 2, 128)
        top = x2[:, 0].reshape(384, 128).astype(F32)
        bot = pltpu.roll(x2[:, 1].reshape(384, 128).astype(F32), 64, 1)
        ret[ab, 0:32, 12:18] = pick(top, bot).astype(BF16).reshape(32, 6, 2, 128)
        ret[ab, 32:64, 12:18] = pick(bot, top).astype(BF16).reshape(32, 6, 2, 128)
        send_back(p, ab, 2 if ab == 1 else 0)

    def wait_back(p, ab, n):
        wait_bytes((mix0, mix1)[p].at[ab, pl.ds(*RET[p][ab][n])], ret_recv.at[p, ab, n])

    def wait_back_sent(p):
        for ab in range(2):
            for n in range(len(RET[p][ab])):
                wait_bytes(ret.at[ab, pl.ds(0, CHIPS - 1), pl.ds(*RET[p][ab][n])], ret_send.at[p, ab, n])

    def mean_rows(values):
        total = jnp.sum(values.reshape(32, 8, 128), 0)
        total = total + pltpu.roll(total, 4, 0)
        total = total + pltpu.roll(total, 2, 0)
        return (total * (1.0 / C)).reshape(1, 8, 128)

    def norm_mix(values, gain):
        centered = values.reshape(32, 8, 128) - mean_rows(values)
        variance = mean_rows(centered * centered)
        return (centered * lax.rsqrt(variance + 1e-05)).reshape(256, 128) * gain

    def finish(p, u):
        mix = (mix0, mix1)[p]
        cols = []
        for e in range(2):
            vals = jnp.concatenate([mix[ab, 2 * u + e].reshape(128, 128) for ab in range(2)], 0).astype(F32)
            cols.append(norm_mix(vals, gain_out[p]).astype(BF16))
        got = jnp.dot(out_a[p], jnp.concatenate(cols, 1), preferred_element_type=F32)
        for e in range(2):
            tp = 2 * u + e
            zt[tp] = (zt[tp].astype(F32) + gate[tp] * got[:, e * 128:(e + 1) * 128]).astype(BF16)

    prepare_in(0)
    for part, (first, last) in enumerate(((0, 6), (6, 9))):
        loads[part].wait()
        rows = slice(*((0, 3072), (3072, 4608))[part])
        work[rows] = pbuf[rows].astype(F32)

        @pl.loop(first, last)
        def _(u):
            for e in range(2):
                load_tiles(2 * u + e, part == 1)
            project(0, u)

    pl.semaphore_wait(barrier, CHIPS)
    send_group(0, 0, 0)
    send_group(0, 1, 0)
    prepare_out(0)
    gates(0)
    prepare_in(1)
    prepare_out(1)
    for ab in range(2):
        mix_out(ab)
        give_back(0, ab)
    wait_sent(0)
    wait_back(0, 0, 0)
    for g in range(3):
        wait_back(0, 1, g)

        @pl.loop(3 * g, 3 * g + 3)
        def _(u):
            finish(0, u)
            project(1, u)

        send_group(1, 0, g)
    send_group(1, 1, 0)
    gates(1)
    wait_back_sent(0)
    for ab in range(2):
        mix_in(ab)
        give_back(1, ab)
    wait_sent(1)
    stores = [
        pltpu.make_async_copy(pbuf.at[pl.ds(a, n)], out.at[pl.ds(a, n)], local.at[2 + i])
        for i, (a, n) in enumerate(((0, 3072), (3072, 1536)))
    ]
    wait_back(1, 0, 0)
    for g in range(3):
        wait_back(1, 1, g)

        @pl.loop(3 * g, 3 * g + 3)
        def _(u):
            finish(1, u)
            for e in range(2):
                store_tiles(2 * u + e, g == 2)

        if g > 0:
            part = g - 1
            rows = slice(*((0, 3072), (3072, 4608))[part])
            pbuf[rows] = work[rows].astype(BF16)
            stores[part].start()
    wait_back_sent(1)
    for store in stores:
        store.wait()


def on_device(pair, norm_in, proj_weight, gate_weight, norm_out, out_weight):
    vmem = pl.BlockSpec(memory_space=pltpu.VMEM)
    hbm = pl.BlockSpec(memory_space=pl.ANY)
    updated = pl.pallas_call(
        kernel,
        out_shape=jax.ShapeDtypeStruct((ROWS * COLS, C), BF16),
        in_specs=[hbm] + [vmem] * 5,
        out_specs=hbm,
        scratch_shapes=[
            pltpu.VMEM((ROWS * COLS, C), BF16),
            pltpu.VMEM((PAIRS, 256, 128), BF16),
            pltpu.VMEM((PAIRS, 256, 128), BF16),
            pltpu.VMEM((PAIRS, 256, 128), F32),
            pltpu.VMEM((4, PAIRS, CHIPS, 2, 128), BF16),
            pltpu.VMEM((4, CHIPS, PAIRS, 2, 128), BF16),
            pltpu.VMEM((4, CHIPS, PAIRS, 2, 128), BF16),
            pltpu.VMEM((2, TOKENS, 384), BF16),
            pltpu.VMEM((2, 384, TOKENS), BF16),
            pltpu.VMEM((2, 384, TOKENS), BF16),
            pltpu.VMEM((2, 2, 2, 192, 384), BF16),
            pltpu.VMEM((2, TOKENS, 384), BF16),
            pltpu.VMEM((2, 2, 192, 384), BF16),
            pltpu.VMEM((2, TOKENS, 384), BF16),
            pltpu.VMEM((3, TOKENS, 128), BF16),
            pltpu.VMEM((2, CHIPS, PAIRS, 2, 128), BF16),
            pltpu.VMEM((2, PAIRS, CHIPS, 2, 128), BF16),
            pltpu.VMEM((2, PAIRS, CHIPS, 2, 128), BF16),
            pltpu.VMEM((ROWS * COLS, 128), F32),
            pltpu.VMEM((1024, 128), F32),
            pltpu.VMEM((1024, 128), F32),
            pltpu.VMEM((2, 1024, 256), BF16),
            pltpu.VMEM((2, 256, 256), BF16),
            pltpu.VMEM((2, 256, 256), BF16),
            pltpu.VMEM((2, 128, 128), F32),
            pltpu.VMEM((2, 256, 128), F32),
            pltpu.VMEM((32, 2, 6, 2, 128), BF16),
            pltpu.SemaphoreType.DMA((2, 2, 3)),
            pltpu.SemaphoreType.DMA((2, 2, 3)),
            pltpu.SemaphoreType.DMA((2, 2, 3)),
            pltpu.SemaphoreType.DMA((2, 2, 3)),
            pltpu.SemaphoreType.DMA((6,)),
            pltpu.SemaphoreType.DMA((6,)),
            pltpu.SemaphoreType.DMA((4,)),
        ],
        compiler_params=pltpu.CompilerParams(
            collective_id=0, has_side_effects=True, vmem_limit_bytes=56 * 2**20
        ),
    )(pair.reshape(ROWS * COLS, C), norm_in, proj_weight, gate_weight, norm_out, out_weight)
    return updated.reshape(ROWS, COLS, C)


def solution(mesh):
    placed = (P("row", "col", None), P(), P(), P(), P(), P())
    return jax.shard_map(
        on_device, mesh=mesh, in_specs=placed, out_specs=P("row", "col", None), check_vma=False
    )
```

```python
import functools

import jax
import jax.numpy as jnp
from jax import lax
from jax.experimental import pallas as pl
from jax.experimental.pallas import tpu as pltpu
from jax.sharding import PartitionSpec as P

F32, BF16 = jnp.float32, jnp.bfloat16
MESH = pl.DeviceIdType.MESH

ROWS, COLS, C = 192, 24, 128
CHIPS = 64
PAIRS = 18
THIRDS = ((0, 6), (6, 6), (12, 6))
FWD = ((THIRDS, ((0, 12), (12, 6))), (THIRDS, ((0, 12), (12, 6))))
RET = ((((0, 18),), THIRDS), (((0, 18),), THIRDS))
TOKENS = 768


def chip_coords():
    row, col = lax.axis_index("row"), lax.axis_index("col")
    return col // 8, (row // 2) * 2 + col % 2, (col // 2) % 4, row % 2


def norm_cols(values, gain):
    mean = jnp.mean(values, 0, keepdims=True)
    centered = values - mean
    variance = jnp.mean(centered * centered, 0, keepdims=True)
    return centered * lax.rsqrt(variance + 1e-05) * gain


def sigmoid(values):
    return 0.5 * jnp.tanh(0.5 * values) + 0.5


def kernel(
    pair, norm_in, proj_w, gate_w, norm_out, out_w, out,
    pbuf, zt, nb, gate, msg, left_right0, left_right1, xl0, xt0, xt0_far, xl1, xr1, xl1_far, xr1_far, mixed, ret, mix0, mix1,
    work, wfa, wfb, proj_a, gate_a, out_a, gain_in, gain_out, x2,
    fwd_send, fwd_recv, ret_send, ret_recv, core_send, core_recv, local,
):
    x, y, z, core = chip_coords()
    y_hi = y // 2
    col = lax.axis_index("col")
    me = y_hi * 32 + col
    sibling = (y_hi * 2 + 1 - core, col)
    y_of = [lax.rem(y + b, 4) for b in range(4)]
    row_of = [v // 2 for v in y_of]
    low_of = [lax.rem(v, 2) for v in y_of]
    z_of = [lax.rem(z + c, 4) * 2 for c in range(4)]

    def pick(a, b):
        return jnp.where(lax.broadcasted_iota(jnp.int32, a.shape, 1) < 64, a, b)

    def each_peer(act):
        @pl.loop(0, 4)
        def _(i):
            for n in range(16):
                b, c = n % 4, (n // 4 + n) % 4
                px = lax.rem(x + (b + c) % 4 + i, 4) * 8

                def one():
                    act(row_of[b], px + low_of[b] + z_of[c])

                if n == 0:
                    pl.when(i > 0)(one)
                else:
                    one()

    def send_all(src_of, dst, send, recv):
        def one(py, pc):
            pltpu.make_async_remote_copy(
                src_ref=src_of(py * 32 + pc), dst_ref=dst, send_sem=send, recv_sem=recv,
                device_id=(py * 2 + core, pc), device_id_type=MESH,
            ).start()

        each_peer(one)
        pltpu.make_async_copy(src_of(me), dst, recv).start()

    def wait_bytes(ref, sem):
        pltpu.make_async_copy(ref, ref, sem).wait()

    loads = [
        pltpu.make_async_copy(pair.at[pl.ds(a, n)], pbuf.at[pl.ds(a, n)], local.at[i])
        for i, (a, n) in enumerate(((0, 3072), (3072, 1536)))
    ]
    for load in loads:
        load.start()

    barrier = pltpu.get_barrier_semaphore()
    pl.semaphore_signal(barrier, inc=1, device_id=sibling, device_id_type=MESH)
    each_peer(lambda py, pc: pl.semaphore_signal(
        barrier, inc=1, device_id=(py * 2 + core, pc), device_id_type=MESH))

    def picked_gain(ref, p):
        rows = lax.broadcasted_iota(jnp.int32, (2, 128), 0) == p
        row = jnp.sum(jnp.where(rows, ref[...], 0.0), 0, keepdims=True)
        return jnp.broadcast_to(row, (128, 128)).T

    def prepare_in(p):
        wt = proj_w[p].astype(F32).T
        wfa[pl.ds(0, 512, stride=2), :] = wt
        wfa[pl.ds(1, 512, stride=2), :] = jnp.zeros_like(wt)
        wfb[pl.ds(0, 512, stride=2), :] = jnp.zeros_like(wt)
        wfb[pl.ds(1, 512, stride=2), :] = wt
        proj_a[p, :, 0:128] = wfa[...].astype(BF16)
        proj_a[p, :, 128:256] = wfb[...].astype(BF16)
        gain_in[p] = picked_gain(norm_in, p)

    def prepare_out(p):
        gt = gate_w[p].astype(F32).T.astype(BF16)
        zero = jnp.zeros((128, 128), BF16)
        gate_a[p, 0:128, 0:128] = gt
        gate_a[p, 0:128, 128:256] = zero
        gate_a[p, 128:256, 0:128] = zero
        gate_a[p, 128:256, 128:256] = gt
        ow = out_w[p].astype(F32)
        for e in range(2):
            wfa[pl.ds(e, 128, stride=2), :] = ow
            wfa[pl.ds(1 - e, 128, stride=2), :] = jnp.zeros_like(ow)
            out_a[p, e * 128:(e + 1) * 128] = wfa[0:256].T.astype(BF16)
        gain = picked_gain(norm_out, p)
        for e in range(2):
            wfa[pl.ds(e, 128, stride=2), :] = gain
        gain_out[p] = wfa[0:256]

    def half_rows(m, first):
        return pl.ds(128 * 24 + m + 12 * first, 64, stride=24)

    def load_tiles(tp, mixed):
        for e in range(2):
            if mixed:
                m = 2 * tp + e - 24
                vals = jnp.concatenate([work[half_rows(m, y_hi), :], work[half_rows(m, 1 - y_hi), :]], 0)
            else:
                vals = work[pl.ds(2 * tp + e, 128, stride=24), :]
            zt[tp, e * 128:(e + 1) * 128] = vals.T.astype(BF16)

    def store_tiles(tp, mixed):
        for e in range(2):
            vals = zt[tp, e * 128:(e + 1) * 128].astype(F32).T
            if mixed:
                m = 2 * tp + e - 24
                work[half_rows(m, y_hi), :] = vals[0:64]
                work[half_rows(m, 1 - y_hi), :] = vals[64:128]
            else:
                work[pl.ds(2 * tp + e, 128, stride=24), :] = vals

    def project(p, u):
        for e in range(2):
            tp = 2 * u + e
            for h in range(2):
                rows = slice(h * 128, (h + 1) * 128)
                nb[tp, rows] = norm_cols(zt[tp, rows].astype(F32), gain_in[p]).astype(BF16)
        n = jnp.concatenate([nb[2 * u], nb[2 * u + 1]], 1)
        for side in range(2):
            a = proj_a[p, side * 512:(side + 1) * 512]
            got = jnp.dot(a, n, preferred_element_type=F32)
            val = (sigmoid(got[256:512]) * got[0:256]).astype(BF16)
            for ab in range(2):
                for e in range(2):
                    block = val[ab * 128:(ab + 1) * 128, e * 128:(e + 1) * 128]
                    msg[ab * 2 + side, 2 * u + e] = block.reshape(64, 2, 128)

    def gates(p):
        @pl.loop(0, 9)
        def _(u):
            n = jnp.concatenate([nb[2 * u], nb[2 * u + 1]], 1)
            g = sigmoid(jnp.dot(gate_a[p], n, preferred_element_type=F32))
            gate[2 * u] = g[:, 0:128]
            gate[2 * u + 1] = g[:, 128:256]

    def span(p, ab, n):
        return pl.ds(*FWD[p][ab][n])

    def send_group(p, ab, n):
        arrived = (left_right0, left_right1)[p]
        both = pl.ds(2 * ab, 2)
        send_all(
            lambda d: msg.at[both, span(p, ab, n), d], arrived.at[both, me, span(p, ab, n)],
            fwd_send.at[p, ab, n], fwd_recv.at[p, ab, n],
        )

    def send_all_b(p):
        for n in range(len(FWD[p][1])):
            send_group(p, 1, n)

    def wait_channel(p, ab, first=0, last=3):
        arrived = (left_right0, left_right1)[p]
        for n in range(len(FWD[p][ab]))[first:last]:
            wait_bytes(arrived.at[pl.ds(2 * ab, 2), :, span(p, ab, n)], fwd_recv.at[p, ab, n])

    def wait_sent(p):
        for ab in range(2):
            for n in range(len(FWD[p][ab])):
                wait_bytes(
                    msg.at[pl.ds(2 * ab, 2), span(p, ab, n), pl.ds(0, CHIPS - 1)], fwd_send.at[p, ab, n])

    def main_cols(src, i, it):
        return src[i, 32 * it:32 * (it + 1), 0:12].reshape(768, 128)

    def mixed_cols(src, i):
        t = src[i, 0:32, 12:18].reshape(384, 128).astype(F32)
        v = src[i, 32:64, 12:18].reshape(384, 128).astype(F32)
        x2[:, 0] = pick(t, v).astype(BF16).reshape(32, 6, 2, 128)
        x2[:, 1] = pltpu.roll(pick(v, t), 64, 1).astype(BF16).reshape(32, 6, 2, 128)
        return x2[...].reshape(768, 128)

    def columns(src, i, tile):
        return main_cols(src, i, tile) if tile < 2 else mixed_cols(src, i)

    def core_copy(src, dst, i):
        return pltpu.make_async_remote_copy(
            src_ref=src, dst_ref=dst, send_sem=core_send.at[i], recv_sem=core_recv.at[i],
            device_id=sibling, device_id_type=MESH,
        )

    def mix_out(ab, arrive):
        src = left_right0
        copies = []
        for part, cols in enumerate((slice(0, 256), slice(256, 384))):
            arrive(part)
            for at in range(cols.start, cols.stop, 128):
                xt0[ab, at:at + 128] = columns(src, ab * 2 + 1, at // 128).T
            rows = pl.ds(cols.start, cols.stop - cols.start)
            copy = core_copy(xt0.at[ab, rows], xt0_far.at[ab, rows], 2 * ab + part)
            copy.start()
            copies.append(copy)
            for at in range(cols.start, cols.stop, 128):
                xl0[ab, :, at:at + 128] = columns(src, ab * 2, at // 128)

        def contract(right, owner):
            got = jnp.dot(right, xl0[ab], preferred_element_type=F32)
            first = pl.multiple_of(owner * 192, 64)
            for it in range(3):
                piece = got[:, it * 128:(it + 1) * 128].astype(BF16)
                mixed[it, pl.ds(first, 128), :] = piece[0:128]
                mixed[it, pl.ds(first + 384, 128), :] = piece[128:256]
                mixed[it, pl.ds(first + 128, 64), :] = piece[256:320]
                mixed[it, pl.ds(first + 512, 64), :] = piece[320:384]

        contract(xt0[ab], core)
        for copy in copies:
            copy.wait()
        contract(xt0_far[ab], 1 - core)

    def own_rows(ref):
        return jnp.concatenate([ref[0, 0:128], ref[1, 0:128], ref[0, 128:192], ref[1, 128:192]], 0)

    def mix_in(ab, arrive):
        src = left_right1
        copies = []
        for part, (first, count) in enumerate(((0, 256), (256, 128))):
            arrive(part)
            cols = pl.ds(first, count)
            for at in range(first, first + count, 128):
                xr1[ab, :, at:at + 128] = columns(src, ab * 2 + 1, at // 128)
            copies.append(core_copy(xr1.at[ab, :, cols], xr1_far.at[ab, :, cols], 4 + 4 * ab + 2 * part))
            copies[-1].start()
            for at in range(first, first + count, 128):
                xl1[ab, :, :, :, at:at + 128] = columns(src, ab * 2, at // 128).reshape(2, 2, 192, 128)
            copies.append(core_copy(
                xl1.at[ab, :, 1 - core, :, cols], xl1_far.at[ab, :, :, cols], 5 + 4 * ab + 2 * part))
            copies[-1].start()

        def contract(right, left):
            return lax.dot_general(right, left, (((1,), (1,)), ((), ())), preferred_element_type=F32)

        got = contract(xr1[ab], own_rows(xl1.at[ab, :, core]))
        for copy in copies:
            copy.wait()
        got = got + contract(xr1_far[ab], own_rows(xl1_far.at[ab]))
        for it in range(3):
            mixed[it] = got[:, it * 128:(it + 1) * 128].astype(BF16)

    def send_back(p, ab, n):
        some = pl.ds(*RET[p][ab][n])
        send_all(
            lambda d: ret.at[ab, d, some], (mix0, mix1)[p].at[ab, some, me],
            ret_send.at[p, ab, n], ret_recv.at[p, ab, n],
        )

    def give_back(p, ab):
        for it in range(2):
            ret[ab, it * 32:(it + 1) * 32, 0:12] = mixed[it].reshape(32, 12, 2, 128)
        if ab == 1:
            send_back(p, ab, 0)
            send_back(p, ab, 1)
        x2[...] = mixed[2].reshape(32, 2, 6, 2, 128)
        top = x2[:, 0].reshape(384, 128).astype(F32)
        bot = pltpu.roll(x2[:, 1].reshape(384, 128).astype(F32), 64, 1)
        ret[ab, 0:32, 12:18] = pick(top, bot).astype(BF16).reshape(32, 6, 2, 128)
        ret[ab, 32:64, 12:18] = pick(bot, top).astype(BF16).reshape(32, 6, 2, 128)
        send_back(p, ab, 2 if ab == 1 else 0)

    def wait_back(p, ab, n):
        wait_bytes((mix0, mix1)[p].at[ab, pl.ds(*RET[p][ab][n])], ret_recv.at[p, ab, n])

    def wait_back_sent(p):
        for ab in range(2):
            for n in range(len(RET[p][ab])):
                wait_bytes(ret.at[ab, pl.ds(0, CHIPS - 1), pl.ds(*RET[p][ab][n])], ret_send.at[p, ab, n])

    def mean_rows(values):
        total = jnp.sum(values.reshape(32, 8, 128), 0)
        total = total + pltpu.roll(total, 4, 0)
        total = total + pltpu.roll(total, 2, 0)
        return (total * (1.0 / C)).reshape(1, 8, 128)

    def norm_mix(values, gain):
        centered = values.reshape(32, 8, 128) - mean_rows(values)
        variance = mean_rows(centered * centered)
        return (centered * lax.rsqrt(variance + 1e-05)).reshape(256, 128) * gain

    def finish(p, u):
        mix = (mix0, mix1)[p]
        cols = []
        for e in range(2):
            vals = jnp.concatenate([mix[ab, 2 * u + e].reshape(128, 128) for ab in range(2)], 0).astype(F32)
            cols.append(norm_mix(vals, gain_out[p]).astype(BF16))
        got = jnp.dot(out_a[p], jnp.concatenate(cols, 1), preferred_element_type=F32)
        for e in range(2):
            tp = 2 * u + e
            zt[tp] = (zt[tp].astype(F32) + gate[tp] * got[:, e * 128:(e + 1) * 128]).astype(BF16)

    def contract_pass(p, mix):
        def second(part):
            wait_channel(p, 1, part, part + 1)
            if part == 0:
                give_back(p, 0)

        mix(0, lambda part: wait_channel(p, 0, 2 * part, 2 + part))
        mix(1, second)
        give_back(p, 1)

    prepare_in(0)
    for g in range(3):
        if g != 1:
            part = g // 2
            loads[part].wait()
            rows = slice(*((0, 3072), (3072, 4608))[part])
            work[rows] = pbuf[rows].astype(F32)

        @pl.loop(3 * g, 3 * g + 3)
        def _(u):
            for e in range(2):
                load_tiles(2 * u + e, g == 2)
            project(0, u)

        if g == 0:
            pl.semaphore_wait(barrier, CHIPS)
        send_group(0, 0, g)
    send_all_b(0)
    prepare_out(0)
    gates(0)
    prepare_in(1)
    prepare_out(1)
    contract_pass(0, mix_out)
    wait_sent(0)
    wait_back(0, 0, 0)
    for g in range(3):
        wait_back(0, 1, g)

        @pl.loop(3 * g, 3 * g + 3)
        def _(u):
            finish(0, u)
            project(1, u)

        send_group(1, 0, g)
    send_all_b(1)
    gates(1)
    wait_back_sent(0)
    contract_pass(1, mix_in)
    wait_sent(1)
    stores = [
        pltpu.make_async_copy(pbuf.at[pl.ds(a, n)], out.at[pl.ds(a, n)], local.at[2 + i])
        for i, (a, n) in enumerate(((0, 3072), (3072, 1536)))
    ]
    wait_back(1, 0, 0)
    for g in range(3):
        wait_back(1, 1, g)

        @pl.loop(3 * g, 3 * g + 3)
        def _(u):
            finish(1, u)
            for e in range(2):
                store_tiles(2 * u + e, g == 2)

        if g > 0:
            part = g - 1
            rows = slice(*((0, 3072), (3072, 4608))[part])
            pbuf[rows] = work[rows].astype(BF16)
            stores[part].start()
    wait_back_sent(1)
    for store in stores:
        store.wait()


def on_device(pair, norm_in, proj_weight, gate_weight, norm_out, out_weight):
    vmem = pl.BlockSpec(memory_space=pltpu.VMEM)
    hbm = pl.BlockSpec(memory_space=pl.ANY)
    updated = pl.pallas_call(
        kernel,
        out_shape=jax.ShapeDtypeStruct((ROWS * COLS, C), BF16),
        in_specs=[hbm] + [vmem] * 5,
        out_specs=hbm,
        scratch_shapes=[
            pltpu.VMEM((ROWS * COLS, C), BF16),
            pltpu.VMEM((PAIRS, 256, 128), BF16),
            pltpu.VMEM((PAIRS, 256, 128), BF16),
            pltpu.VMEM((PAIRS, 256, 128), F32),
            pltpu.VMEM((4, PAIRS, CHIPS, 2, 128), BF16),
            pltpu.VMEM((4, CHIPS, PAIRS, 2, 128), BF16),
            pltpu.VMEM((4, CHIPS, PAIRS, 2, 128), BF16),
            pltpu.VMEM((2, TOKENS, 384), BF16),
            pltpu.VMEM((2, 384, TOKENS), BF16),
            pltpu.VMEM((2, 384, TOKENS), BF16),
            pltpu.VMEM((2, 2, 2, 192, 384), BF16),
            pltpu.VMEM((2, TOKENS, 384), BF16),
            pltpu.VMEM((2, 2, 192, 384), BF16),
            pltpu.VMEM((2, TOKENS, 384), BF16),
            pltpu.VMEM((3, TOKENS, 128), BF16),
            pltpu.VMEM((2, CHIPS, PAIRS, 2, 128), BF16),
            pltpu.VMEM((2, PAIRS, CHIPS, 2, 128), BF16),
            pltpu.VMEM((2, PAIRS, CHIPS, 2, 128), BF16),
            pltpu.VMEM((ROWS * COLS, 128), F32),
            pltpu.VMEM((1024, 128), F32),
            pltpu.VMEM((1024, 128), F32),
            pltpu.VMEM((2, 1024, 256), BF16),
            pltpu.VMEM((2, 256, 256), BF16),
            pltpu.VMEM((2, 256, 256), BF16),
            pltpu.VMEM((2, 128, 128), F32),
            pltpu.VMEM((2, 256, 128), F32),
            pltpu.VMEM((32, 2, 6, 2, 128), BF16),
            pltpu.SemaphoreType.DMA((2, 2, 3)),
            pltpu.SemaphoreType.DMA((2, 2, 3)),
            pltpu.SemaphoreType.DMA((2, 2, 3)),
            pltpu.SemaphoreType.DMA((2, 2, 3)),
            pltpu.SemaphoreType.DMA((12,)),
            pltpu.SemaphoreType.DMA((12,)),
            pltpu.SemaphoreType.DMA((4,)),
        ],
        compiler_params=pltpu.CompilerParams(
            collective_id=0, has_side_effects=True, vmem_limit_bytes=56 * 2**20
        ),
    )(pair.reshape(ROWS * COLS, C), norm_in, proj_weight, gate_weight, norm_out, out_weight)
    return updated.reshape(ROWS, COLS, C)


def solution(mesh):
    placed = (P("row", "col", None), P(), P(), P(), P(), P())
    return jax.shard_map(
        on_device, mesh=mesh, in_specs=placed, out_specs=P("row", "col", None), check_vma=False
    )
```

```python
import functools

import jax
import jax.numpy as jnp
from jax import lax
from jax.experimental import pallas as pl
from jax.experimental.pallas import tpu as pltpu
from jax.sharding import PartitionSpec as P

F32, BF16 = jnp.float32, jnp.bfloat16
MESH = pl.DeviceIdType.MESH

ROWS, COLS, C = 192, 24, 128
CHIPS = 64
PAIRS = 18
THIRDS = ((0, 6), (6, 6), (12, 6))
FWD = ((THIRDS, ((0, 12), (12, 6))), (THIRDS, ((0, 12), (12, 6))))
RET = ((((0, 18),), THIRDS), (((0, 18),), THIRDS))
TOKENS = 768


def chip_coords():
    row, col = lax.axis_index("row"), lax.axis_index("col")
    return col // 8, (row // 2) * 2 + col % 2, (col // 2) % 4, row % 2


def norm_cols(values, gain):
    mean = jnp.mean(values, 0, keepdims=True)
    centered = values - mean
    variance = jnp.mean(centered * centered, 0, keepdims=True)
    return centered * lax.rsqrt(variance + 1e-05) * gain


def sigmoid(values):
    return 0.5 * jnp.tanh(0.5 * values) + 0.5


def kernel(
    pair, norm_in, proj_w, gate_w, norm_out, out_w, out,
    pbuf, zt, nb, gate, msg, left_right0, left_right1, xl0, xt0, xt0_far, xl1, xr1, xl1_far, xr1_far, mixed, ret, mix0, mix1,
    work, wfa, wfb, proj_a, gate_a, out_a, gain_in, gain_out, x2,
    fwd_send, fwd_recv, ret_send, ret_recv, core_send, core_recv, local,
):
    x, y, z, core = chip_coords()
    y_hi = y // 2
    col = lax.axis_index("col")
    me = y_hi * 32 + col
    sibling = (y_hi * 2 + 1 - core, col)
    y_of = [lax.rem(y + b, 4) for b in range(4)]
    row_of = [v // 2 for v in y_of]
    low_of = [lax.rem(v, 2) for v in y_of]
    z_of = [lax.rem(z + c, 4) * 2 for c in range(4)]

    def pick(a, b):
        return jnp.where(lax.broadcasted_iota(jnp.int32, a.shape, 1) < 64, a, b)

    def each_peer(act):
        @pl.loop(0, 4)
        def _(i):
            for n in range(16):
                b, c = n % 4, (n // 4 + n) % 4
                px = lax.rem(x + (b + c) % 4 + i, 4) * 8

                def one():
                    act(row_of[b], px + low_of[b] + z_of[c])

                if n == 0:
                    pl.when(i > 0)(one)
                else:
                    one()

    def send_all(src_of, dst, send, recv):
        def one(py, pc):
            pltpu.make_async_remote_copy(
                src_ref=src_of(py * 32 + pc), dst_ref=dst, send_sem=send, recv_sem=recv,
                device_id=(py * 2 + core, pc), device_id_type=MESH,
            ).start()

        each_peer(one)
        pltpu.make_async_copy(src_of(me), dst, recv).start()

    def wait_bytes(ref, sem):
        pltpu.make_async_copy(ref, ref, sem).wait()

    loads = [
        pltpu.make_async_copy(pair.at[pl.ds(a, n)], pbuf.at[pl.ds(a, n)], local.at[i])
        for i, (a, n) in enumerate(((0, 3072), (3072, 1536)))
    ]
    for load in loads:
        load.start()

    barrier = pltpu.get_barrier_semaphore()
    pl.semaphore_signal(barrier, inc=1, device_id=sibling, device_id_type=MESH)
    each_peer(lambda py, pc: pl.semaphore_signal(
        barrier, inc=1, device_id=(py * 2 + core, pc), device_id_type=MESH))

    def picked_gain(ref, p):
        rows = lax.broadcasted_iota(jnp.int32, (2, 128), 0) == p
        row = jnp.sum(jnp.where(rows, ref[...], 0.0), 0, keepdims=True)
        return jnp.broadcast_to(row, (128, 128)).T

    def prepare_in(p):
        wt = proj_w[p].astype(F32).T
        wfa[pl.ds(0, 512, stride=2), :] = wt
        wfa[pl.ds(1, 512, stride=2), :] = jnp.zeros_like(wt)
        wfb[pl.ds(0, 512, stride=2), :] = jnp.zeros_like(wt)
        wfb[pl.ds(1, 512, stride=2), :] = wt
        proj_a[p, :, 0:128] = wfa[...].astype(BF16)
        proj_a[p, :, 128:256] = wfb[...].astype(BF16)
        gain_in[p] = picked_gain(norm_in, p)

    def prepare_out(p):
        gt = gate_w[p].astype(F32).T.astype(BF16)
        zero = jnp.zeros((128, 128), BF16)
        gate_a[p, 0:128, 0:128] = gt
        gate_a[p, 0:128, 128:256] = zero
        gate_a[p, 128:256, 0:128] = zero
        gate_a[p, 128:256, 128:256] = gt
        ow = out_w[p].astype(F32)
        for e in range(2):
            wfa[pl.ds(e, 128, stride=2), :] = ow
            wfa[pl.ds(1 - e, 128, stride=2), :] = jnp.zeros_like(ow)
            out_a[p, e * 128:(e + 1) * 128] = wfa[0:256].T.astype(BF16)
        gain = picked_gain(norm_out, p)
        for e in range(2):
            wfa[pl.ds(e, 128, stride=2), :] = gain
        gain_out[p] = wfa[0:256]

    def half_rows(m, first):
        return pl.ds(128 * 24 + m + 12 * first, 64, stride=24)

    def load_tiles(tp, mixed):
        for e in range(2):
            if mixed:
                m = 2 * tp + e - 24
                vals = jnp.concatenate([work[half_rows(m, y_hi), :], work[half_rows(m, 1 - y_hi), :]], 0)
            else:
                vals = work[pl.ds(2 * tp + e, 128, stride=24), :]
            zt[tp, e * 128:(e + 1) * 128] = vals.T.astype(BF16)

    def store_tiles(tp, mixed):
        for e in range(2):
            vals = zt[tp, e * 128:(e + 1) * 128].astype(F32).T
            if mixed:
                m = 2 * tp + e - 24
                work[half_rows(m, y_hi), :] = vals[0:64]
                work[half_rows(m, 1 - y_hi), :] = vals[64:128]
            else:
                work[pl.ds(2 * tp + e, 128, stride=24), :] = vals

    def project(p, u):
        for e in range(2):
            tp = 2 * u + e
            for h in range(2):
                rows = slice(h * 128, (h + 1) * 128)
                nb[tp, rows] = norm_cols(zt[tp, rows].astype(F32), gain_in[p]).astype(BF16)
        n = jnp.concatenate([nb[2 * u], nb[2 * u + 1]], 1)
        for side in range(2):
            a = proj_a[p, side * 512:(side + 1) * 512]
            got = jnp.dot(a, n, preferred_element_type=F32)
            val = (sigmoid(got[256:512]) * got[0:256]).astype(BF16)
            for ab in range(2):
                for e in range(2):
                    block = val[ab * 128:(ab + 1) * 128, e * 128:(e + 1) * 128]
                    msg[ab * 2 + side, 2 * u + e] = block.reshape(64, 2, 128)

    def gates(p):
        @pl.loop(0, 9)
        def _(u):
            n = jnp.concatenate([nb[2 * u], nb[2 * u + 1]], 1)
            g = sigmoid(jnp.dot(gate_a[p], n, preferred_element_type=F32))
            gate[2 * u] = g[:, 0:128]
            gate[2 * u + 1] = g[:, 128:256]

    def span(p, ab, n):
        return pl.ds(*FWD[p][ab][n])

    def send_group(p, ab, n):
        arrived = (left_right0, left_right1)[p]
        both = pl.ds(2 * ab, 2)
        send_all(
            lambda d: msg.at[both, span(p, ab, n), d], arrived.at[both, me, span(p, ab, n)],
            fwd_send.at[p, ab, n], fwd_recv.at[p, ab, n],
        )

    def send_all_b(p):
        for n in range(len(FWD[p][1])):
            send_group(p, 1, n)

    def wait_channel(p, ab, first=0, last=3):
        arrived = (left_right0, left_right1)[p]
        for n in range(len(FWD[p][ab]))[first:last]:
            wait_bytes(arrived.at[pl.ds(2 * ab, 2), :, span(p, ab, n)], fwd_recv.at[p, ab, n])

    def wait_sent(p):
        for ab in range(2):
            for n in range(len(FWD[p][ab])):
                wait_bytes(
                    msg.at[pl.ds(2 * ab, 2), span(p, ab, n), pl.ds(0, CHIPS - 1)], fwd_send.at[p, ab, n])

    def main_cols(src, i, it):
        return src[i, 32 * it:32 * (it + 1), 0:12].reshape(768, 128)

    def mixed_cols(src, i):
        t = src[i, 0:32, 12:18].reshape(384, 128).astype(F32)
        v = src[i, 32:64, 12:18].reshape(384, 128).astype(F32)
        x2[:, 0] = pick(t, v).astype(BF16).reshape(32, 6, 2, 128)
        x2[:, 1] = pltpu.roll(pick(v, t), 64, 1).astype(BF16).reshape(32, 6, 2, 128)
        return x2[...].reshape(768, 128)

    def columns(src, i, tile):
        return main_cols(src, i, tile) if tile < 2 else mixed_cols(src, i)

    def core_copy(src, dst, i):
        return pltpu.make_async_remote_copy(
            src_ref=src, dst_ref=dst, send_sem=core_send.at[i], recv_sem=core_recv.at[i],
            device_id=sibling, device_id_type=MESH,
        )

    def mix_out(ab, arrive):
        src = left_right0
        copies = []
        for part, cols in enumerate((slice(0, 256), slice(256, 384))):
            arrive(part)
            for at in range(cols.start, cols.stop, 128):
                xt0[ab, at:at + 128] = columns(src, ab * 2 + 1, at // 128).T
            rows = pl.ds(cols.start, cols.stop - cols.start)
            copy = core_copy(xt0.at[ab, rows], xt0_far.at[ab, rows], 2 * ab + part)
            copy.start()
            copies.append(copy)
            for at in range(cols.start, cols.stop, 128):
                xl0[ab, :, at:at + 128] = columns(src, ab * 2, at // 128)

        def contract(right, owner):
            got = jnp.dot(right, xl0[ab], preferred_element_type=F32)
            first = pl.multiple_of(owner * 192, 64)
            for it in range(3):
                piece = got[:, it * 128:(it + 1) * 128].astype(BF16)
                mixed[it, pl.ds(first, 128), :] = piece[0:128]
                mixed[it, pl.ds(first + 384, 128), :] = piece[128:256]
                mixed[it, pl.ds(first + 128, 64), :] = piece[256:320]
                mixed[it, pl.ds(first + 512, 64), :] = piece[320:384]

        contract(xt0[ab], core)
        for copy in copies:
            copy.wait()
        contract(xt0_far[ab], 1 - core)

    def own_rows(ref):
        return jnp.concatenate([ref[0, 0:128], ref[1, 0:128], ref[0, 128:192], ref[1, 128:192]], 0)

    def mix_in(ab, arrive):
        src = left_right1
        copies = []
        for part, (first, count) in enumerate(((0, 256), (256, 128))):
            arrive(part)
            cols = pl.ds(first, count)
            for at in range(first, first + count, 128):
                xr1[ab, :, at:at + 128] = columns(src, ab * 2 + 1, at // 128)
            copies.append(core_copy(xr1.at[ab, :, cols], xr1_far.at[ab, :, cols], 4 + 4 * ab + 2 * part))
            copies[-1].start()
            for at in range(first, first + count, 128):
                xl1[ab, :, :, :, at:at + 128] = columns(src, ab * 2, at // 128).reshape(2, 2, 192, 128)
            copies.append(core_copy(
                xl1.at[ab, :, 1 - core, :, cols], xl1_far.at[ab, :, :, cols], 5 + 4 * ab + 2 * part))
            copies[-1].start()

        def contract(right, left):
            return lax.dot_general(right, left, (((1,), (1,)), ((), ())), preferred_element_type=F32)

        got = contract(xr1[ab], own_rows(xl1.at[ab, :, core]))
        for copy in copies:
            copy.wait()
        got = got + contract(xr1_far[ab], own_rows(xl1_far.at[ab]))
        for it in range(3):
            mixed[it] = got[:, it * 128:(it + 1) * 128].astype(BF16)

    def send_back(p, ab, n):
        some = pl.ds(*RET[p][ab][n])
        send_all(
            lambda d: ret.at[ab, d, some], (mix0, mix1)[p].at[ab, some, me],
            ret_send.at[p, ab, n], ret_recv.at[p, ab, n],
        )

    def give_back(p, ab):
        for it in range(2):
            ret[ab, it * 32:(it + 1) * 32, 0:12] = mixed[it].reshape(32, 12, 2, 128)
        if ab == 1:
            send_back(p, ab, 0)
            send_back(p, ab, 1)
        x2[...] = mixed[2].reshape(32, 2, 6, 2, 128)
        top = x2[:, 0].reshape(384, 128).astype(F32)
        bot = pltpu.roll(x2[:, 1].reshape(384, 128).astype(F32), 64, 1)
        ret[ab, 0:32, 12:18] = pick(top, bot).astype(BF16).reshape(32, 6, 2, 128)
        ret[ab, 32:64, 12:18] = pick(bot, top).astype(BF16).reshape(32, 6, 2, 128)
        send_back(p, ab, 2 if ab == 1 else 0)

    def wait_back(p, ab, n):
        wait_bytes((mix0, mix1)[p].at[ab, pl.ds(*RET[p][ab][n])], ret_recv.at[p, ab, n])

    def wait_back_sent(p):
        for ab in range(2):
            for n in range(len(RET[p][ab])):
                wait_bytes(ret.at[ab, pl.ds(0, CHIPS - 1), pl.ds(*RET[p][ab][n])], ret_send.at[p, ab, n])

    def mean_rows(values):
        total = jnp.sum(values.reshape(32, 8, 128), 0)
        total = total + pltpu.roll(total, 4, 0)
        total = total + pltpu.roll(total, 2, 0)
        return (total * (1.0 / C)).reshape(1, 8, 128)

    def norm_mix(values, gain):
        centered = values.reshape(32, 8, 128) - mean_rows(values)
        variance = mean_rows(centered * centered)
        return (centered * lax.rsqrt(variance + 1e-05)).reshape(256, 128) * gain

    def finish(p, u):
        mix = (mix0, mix1)[p]
        cols = []
        for e in range(2):
            vals = jnp.concatenate([mix[ab, 2 * u + e].reshape(128, 128) for ab in range(2)], 0).astype(F32)
            cols.append(norm_mix(vals, gain_out[p]).astype(BF16))
        got = jnp.dot(out_a[p], jnp.concatenate(cols, 1), preferred_element_type=F32)
        for e in range(2):
            tp = 2 * u + e
            zt[tp] = (zt[tp].astype(F32) + gate[tp] * got[:, e * 128:(e + 1) * 128]).astype(BF16)

    def contract_pass(p, mix):
        def second(part):
            wait_channel(p, 1, part, part + 1)
            if part == 0:
                give_back(p, 0)

        mix(0, lambda part: wait_channel(p, 0, 2 * part, 2 + part))
        mix(1, second)
        give_back(p, 1)

    prepare_in(0)
    for g in range(3):
        if g != 1:
            part = g // 2
            loads[part].wait()
            rows = slice(*((0, 3072), (3072, 4608))[part])
            work[rows] = pbuf[rows].astype(F32)

        @pl.loop(3 * g, 3 * g + 3)
        def _(u):
            for e in range(2):
                load_tiles(2 * u + e, g == 2)
            project(0, u)

        if g == 0:
            pl.semaphore_wait(barrier, CHIPS)
        send_group(0, 0, g)
    send_all_b(0)
    prepare_out(0)
    gates(0)
    prepare_in(1)
    prepare_out(1)
    contract_pass(0, mix_out)
    wait_sent(0)
    wait_back(0, 0, 0)
    for g in range(3):
        wait_back(0, 1, g)

        @pl.loop(3 * g, 3 * g + 3)
        def _(u):
            finish(0, u)
            project(1, u)

        send_group(1, 0, g)
    send_all_b(1)
    gates(1)
    wait_back_sent(0)
    contract_pass(1, mix_in)
    wait_sent(1)
    wait_back(1, 0, 0)
    for g in range(3):
        wait_back(1, 1, g)

        @pl.loop(3 * g, 3 * g + 3)
        def _(u):
            finish(1, u)
            for e in range(2):
                store_tiles(2 * u + e, g == 2)

        if g > 0:
            part = g - 1
            rows = slice(*((0, 3072), (3072, 4608))[part])
            out[rows] = work[rows].astype(BF16)
    wait_back_sent(1)


def on_device(pair, norm_in, proj_weight, gate_weight, norm_out, out_weight):
    vmem = pl.BlockSpec(memory_space=pltpu.VMEM)
    hbm = pl.BlockSpec(memory_space=pl.ANY)
    updated = pl.pallas_call(
        kernel,
        out_shape=pltpu.VMEM((ROWS * COLS, C), BF16),
        in_specs=[hbm] + [vmem] * 5,
        out_specs=vmem,
        scratch_shapes=[
            pltpu.VMEM((ROWS * COLS, C), BF16),
            pltpu.VMEM((PAIRS, 256, 128), BF16),
            pltpu.VMEM((PAIRS, 256, 128), BF16),
            pltpu.VMEM((PAIRS, 256, 128), F32),
            pltpu.VMEM((4, PAIRS, CHIPS, 2, 128), BF16),
            pltpu.VMEM((4, CHIPS, PAIRS, 2, 128), BF16),
            pltpu.VMEM((4, CHIPS, PAIRS, 2, 128), BF16),
            pltpu.VMEM((2, TOKENS, 384), BF16),
            pltpu.VMEM((2, 384, TOKENS), BF16),
            pltpu.VMEM((2, 384, TOKENS), BF16),
            pltpu.VMEM((2, 2, 2, 192, 384), BF16),
            pltpu.VMEM((2, TOKENS, 384), BF16),
            pltpu.VMEM((2, 2, 192, 384), BF16),
            pltpu.VMEM((2, TOKENS, 384), BF16),
            pltpu.VMEM((3, TOKENS, 128), BF16),
            pltpu.VMEM((2, CHIPS, PAIRS, 2, 128), BF16),
            pltpu.VMEM((2, PAIRS, CHIPS, 2, 128), BF16),
            pltpu.VMEM((2, PAIRS, CHIPS, 2, 128), BF16),
            pltpu.VMEM((ROWS * COLS, 128), F32),
            pltpu.VMEM((1024, 128), F32),
            pltpu.VMEM((1024, 128), F32),
            pltpu.VMEM((2, 1024, 256), BF16),
            pltpu.VMEM((2, 256, 256), BF16),
            pltpu.VMEM((2, 256, 256), BF16),
            pltpu.VMEM((2, 128, 128), F32),
            pltpu.VMEM((2, 256, 128), F32),
            pltpu.VMEM((32, 2, 6, 2, 128), BF16),
            pltpu.SemaphoreType.DMA((2, 2, 3)),
            pltpu.SemaphoreType.DMA((2, 2, 3)),
            pltpu.SemaphoreType.DMA((2, 2, 3)),
            pltpu.SemaphoreType.DMA((2, 2, 3)),
            pltpu.SemaphoreType.DMA((12,)),
            pltpu.SemaphoreType.DMA((12,)),
            pltpu.SemaphoreType.DMA((2,)),
        ],
        compiler_params=pltpu.CompilerParams(
            collective_id=0, has_side_effects=True, vmem_limit_bytes=60 * 2**20
        ),
    )(pair.reshape(ROWS * COLS, C), norm_in, proj_weight, gate_weight, norm_out, out_weight)
    return updated.reshape(ROWS, COLS, C)


def solution(mesh):
    placed = (P("row", "col", None), P(), P(), P(), P(), P())
    return jax.shard_map(
        on_device, mesh=mesh, in_specs=placed, out_specs=P("row", "col", None), check_vma=False
    )
```

```python
import functools

import jax
import jax.numpy as jnp
from jax import lax
from jax.experimental import pallas as pl
from jax.experimental.pallas import tpu as pltpu
from jax.sharding import PartitionSpec as P

F32, BF16 = jnp.float32, jnp.bfloat16
MESH = pl.DeviceIdType.MESH

ROWS, COLS, C = 192, 24, 128
CHIPS = 64
PAIRS = 18
THIRDS = ((0, 6), (6, 6), (12, 6))
FWD = ((THIRDS, ((0, 12), (12, 6))), (((0, 2), (2, 4), (6, 6), (12, 6)), ((0, 12), (12, 6))))
RET = ((((0, 18),), ((0, 2), (2, 4), (6, 6), (12, 6))), (((0, 18),), THIRDS))
TOKENS = 768


def chip_coords():
    row, col = lax.axis_index("row"), lax.axis_index("col")
    return col // 8, (row // 2) * 2 + col % 2, (col // 2) % 4, row % 2


def norm_cols(values, gain):
    mean = jnp.mean(values, 0, keepdims=True)
    centered = values - mean
    variance = jnp.mean(centered * centered, 0, keepdims=True)
    return centered * lax.rsqrt(variance + 1e-05) * gain


def sigmoid(values):
    return 0.5 * jnp.tanh(0.5 * values) + 0.5


def kernel(
    pair, norm_in_hbm, proj_hbm, gate_hbm, norm_out_hbm, out_hbm, out,
    norm_in, proj_w, gate_w, norm_out, out_w,
    pbuf, zt, nb, gate, msg, left_right0, left_right1, xl0, xt0, xt0_far, xl1, xr1, xl1_far, xr1_far, mixed, ret, mix0, mix1,
    work, wfa, wfb, proj_a, gate_a, out_a, gain_in, gain_out, x2,
    fwd_send, fwd_recv, ret_send, ret_recv, core_send, core_recv, local,
):
    x, y, z, core = chip_coords()
    y_hi = y // 2
    col = lax.axis_index("col")
    me = y_hi * 32 + col
    sibling = (y_hi * 2 + 1 - core, col)
    y_of = [lax.rem(y + b, 4) for b in range(4)]
    row_of = [v // 2 for v in y_of]
    low_of = [lax.rem(v, 2) for v in y_of]
    z_of = [lax.rem(z + c, 4) * 2 for c in range(4)]

    def pick(a, b):
        return jnp.where(lax.broadcasted_iota(jnp.int32, a.shape, 1) < 64, a, b)

    def each_peer(act):
        @pl.loop(0, 4)
        def _(i):
            for n in range(16):
                b, c = n % 4, (n // 4 + n) % 4
                px = lax.rem(x + (b + c) % 4 + i, 4) * 8

                def one():
                    act(row_of[b], px + low_of[b] + z_of[c])

                if n == 0:
                    pl.when(i > 0)(one)
                else:
                    one()

    def send_all(src_of, dst, send, recv):
        def one(py, pc):
            pltpu.make_async_remote_copy(
                src_ref=src_of(py * 32 + pc), dst_ref=dst, send_sem=send, recv_sem=recv,
                device_id=(py * 2 + core, pc), device_id_type=MESH,
            ).start()

        each_peer(one)
        pltpu.make_async_copy(src_of(me), dst, recv).start()

    def wait_bytes(ref, sem):
        pltpu.make_async_copy(ref, ref, sem).wait()

    barrier = pltpu.get_barrier_semaphore()
    pl.semaphore_signal(barrier, inc=1, device_id=sibling, device_id_type=MESH)
    each_peer(lambda py, pc: pl.semaphore_signal(
        barrier, inc=1, device_id=(py * 2 + core, pc), device_id_type=MESH))

    loads = [
        pltpu.make_async_copy(pair.at[pl.ds(a, n)], pbuf.at[pl.ds(a, n)], local.at[i])
        for i, (a, n) in enumerate(((0, 3072), (3072, 1536)))
    ]
    weights = [
        pltpu.make_async_copy(src, dst, local.at[2 + i])
        for i, (src, dst) in enumerate((
            (norm_in_hbm, norm_in), (proj_hbm, proj_w), (gate_hbm, gate_w), (norm_out_hbm, norm_out), (out_hbm, out_w)))
    ]
    for load in weights[:2] + loads + weights[2:]:
        load.start()

    def picked_gain(ref, p):
        rows = lax.broadcasted_iota(jnp.int32, (2, 128), 0) == p
        row = jnp.sum(jnp.where(rows, ref[...], 0.0), 0, keepdims=True)
        return jnp.broadcast_to(row, (128, 128)).T

    def prepare_in(p):
        wt = proj_w[p].astype(F32).T
        wfa[pl.ds(0, 512, stride=2), :] = wt
        wfa[pl.ds(1, 512, stride=2), :] = jnp.zeros_like(wt)
        wfb[pl.ds(0, 512, stride=2), :] = jnp.zeros_like(wt)
        wfb[pl.ds(1, 512, stride=2), :] = wt
        proj_a[p, :, 0:128] = wfa[...].astype(BF16)
        proj_a[p, :, 128:256] = wfb[...].astype(BF16)
        gain_in[p] = picked_gain(norm_in, p)

    def prepare_out(p):
        gt = gate_w[p].astype(F32).T.astype(BF16)
        zero = jnp.zeros((128, 128), BF16)
        gate_a[p, 0:128, 0:128] = gt
        gate_a[p, 0:128, 128:256] = zero
        gate_a[p, 128:256, 0:128] = zero
        gate_a[p, 128:256, 128:256] = gt
        ow = out_w[p].astype(F32)
        for e in range(2):
            wfa[pl.ds(e, 128, stride=2), :] = ow
            wfa[pl.ds(1 - e, 128, stride=2), :] = jnp.zeros_like(ow)
            out_a[p, e * 128:(e + 1) * 128] = wfa[0:256].T.astype(BF16)
        gain = picked_gain(norm_out, p)
        for e in range(2):
            wfa[pl.ds(e, 128, stride=2), :] = gain
        gain_out[p] = wfa[0:256]

    def half_rows(m, first):
        return pl.ds(128 * 24 + m + 12 * first, 64, stride=24)

    def load_tiles(tp, mixed):
        for e in range(2):
            if mixed:
                m = 2 * tp + e - 24
                vals = jnp.concatenate([work[half_rows(m, y_hi), :], work[half_rows(m, 1 - y_hi), :]], 0)
            else:
                vals = work[pl.ds(2 * tp + e, 128, stride=24), :]
            zt[tp, e * 128:(e + 1) * 128] = vals.T.astype(BF16)

    def store_tiles(tp, mixed):
        for e in range(2):
            vals = zt[tp, e * 128:(e + 1) * 128].astype(F32).T
            if mixed:
                m = 2 * tp + e - 24
                work[half_rows(m, y_hi), :] = vals[0:64]
                work[half_rows(m, 1 - y_hi), :] = vals[64:128]
            else:
                work[pl.ds(2 * tp + e, 128, stride=24), :] = vals

    def project(p, u):
        for e in range(2):
            tp = 2 * u + e
            for h in range(2):
                rows = slice(h * 128, (h + 1) * 128)
                nb[tp, rows] = norm_cols(zt[tp, rows].astype(F32), gain_in[p]).astype(BF16)
        n = jnp.concatenate([nb[2 * u], nb[2 * u + 1]], 1)
        for side in range(2):
            a = proj_a[p, side * 512:(side + 1) * 512]
            got = jnp.dot(a, n, preferred_element_type=F32)
            val = (sigmoid(got[256:512]) * got[0:256]).astype(BF16)
            for ab in range(2):
                for e in range(2):
                    block = val[ab * 128:(ab + 1) * 128, e * 128:(e + 1) * 128]
                    msg[ab * 2 + side, 2 * u + e] = block.reshape(64, 2, 128)

    def gates(p):
        @pl.loop(0, 9)
        def _(u):
            n = jnp.concatenate([nb[2 * u], nb[2 * u + 1]], 1)
            g = sigmoid(jnp.dot(gate_a[p], n, preferred_element_type=F32))
            gate[2 * u] = g[:, 0:128]
            gate[2 * u + 1] = g[:, 128:256]

    def span(p, ab, n):
        return pl.ds(*FWD[p][ab][n])

    def send_group(p, ab, n):
        arrived = (left_right0, left_right1)[p]
        both = pl.ds(2 * ab, 2)
        send_all(
            lambda d: msg.at[both, span(p, ab, n), d], arrived.at[both, me, span(p, ab, n)],
            fwd_send.at[p, ab, n], fwd_recv.at[p, ab, n],
        )

    def send_all_b(p):
        for n in range(len(FWD[p][1])):
            send_group(p, 1, n)

    def wait_channel(p, ab, first=0, last=4):
        arrived = (left_right0, left_right1)[p]
        for n in range(len(FWD[p][ab]))[first:last]:
            wait_bytes(arrived.at[pl.ds(2 * ab, 2), :, span(p, ab, n)], fwd_recv.at[p, ab, n])

    def wait_sent(p):
        for ab in range(2):
            for n in range(len(FWD[p][ab])):
                wait_bytes(
                    msg.at[pl.ds(2 * ab, 2), span(p, ab, n), pl.ds(0, CHIPS - 1)], fwd_send.at[p, ab, n])

    def main_cols(src, i, it):
        return src[i, 32 * it:32 * (it + 1), 0:12].reshape(768, 128)

    def mixed_cols(src, i):
        t = src[i, 0:32, 12:18].reshape(384, 128).astype(F32)
        v = src[i, 32:64, 12:18].reshape(384, 128).astype(F32)
        x2[:, 0] = pick(t, v).astype(BF16).reshape(32, 6, 2, 128)
        x2[:, 1] = pltpu.roll(pick(v, t), 64, 1).astype(BF16).reshape(32, 6, 2, 128)
        return x2[...].reshape(768, 128)

    def columns(src, i, tile):
        return main_cols(src, i, tile) if tile < 2 else mixed_cols(src, i)

    def core_copy(src, dst, i):
        return pltpu.make_async_remote_copy(
            src_ref=src, dst_ref=dst, send_sem=core_send.at[i], recv_sem=core_recv.at[i],
            device_id=sibling, device_id_type=MESH,
        )

    def mix_out(ab, arrive):
        src = left_right0
        copies = []
        for part, cols in enumerate((slice(0, 256), slice(256, 384))):
            arrive(part)
            for at in range(cols.start, cols.stop, 128):
                xt0[ab, at:at + 128] = columns(src, ab * 2 + 1, at // 128).T
            rows = pl.ds(cols.start, cols.stop - cols.start)
            copy = core_copy(xt0.at[ab, rows], xt0_far.at[ab, rows], 2 * ab + part)
            copy.start()
            copies.append(copy)
            for at in range(cols.start, cols.stop, 128):
                xl0[ab, :, at:at + 128] = columns(src, ab * 2, at // 128)

        def contract(right, owner, tiles):
            first = pl.multiple_of(owner * 192, 64)
            got = jnp.dot(right[ab, tiles[0] * 128:(tiles[-1] + 1) * 128], xl0[ab], preferred_element_type=F32)
            for it in range(3):
                for n, tile in enumerate(tiles):
                    piece = got[n * 128:(n + 1) * 128, it * 128:(it + 1) * 128].astype(BF16)
                    if tile < 2:
                        mixed[it, pl.ds(first + 384 * tile, 128), :] = piece
                    else:
                        mixed[it, pl.ds(first + 128, 64), :] = piece[0:64]
                        mixed[it, pl.ds(first + 512, 64), :] = piece[64:128]

        contract(xt0, core, (0, 1, 2))
        copies[0].wait()
        contract(xt0_far, 1 - core, (0, 1))
        copies[1].wait()
        contract(xt0_far, 1 - core, (2,))

    def own_rows(ref):
        return jnp.concatenate([ref[0, 0:128], ref[1, 0:128], ref[0, 128:192], ref[1, 128:192]], 0)

    def mix_in(ab, arrive):
        src = left_right1
        copies = []
        for part, (first, count) in enumerate(((0, 256), (256, 128))):
            arrive(part)
            cols = pl.ds(first, count)
            for at in range(first, first + count, 128):
                xr1[ab, :, at:at + 128] = columns(src, ab * 2 + 1, at // 128)
            copies.append(core_copy(xr1.at[ab, :, cols], xr1_far.at[ab, :, cols], 4 + 4 * ab + 2 * part))
            copies[-1].start()
            for at in range(first, first + count, 128):
                xl1[ab, :, :, :, at:at + 128] = columns(src, ab * 2, at // 128).reshape(2, 2, 192, 128)
            copies.append(core_copy(
                xl1.at[ab, :, 1 - core, :, cols], xl1_far.at[ab, :, :, cols], 5 + 4 * ab + 2 * part))
            copies[-1].start()

        def contract(right, left):
            return lax.dot_general(right, left, (((1,), (1,)), ((), ())), preferred_element_type=F32)

        got = contract(xr1[ab], own_rows(xl1.at[ab, :, core]))
        for part, cols in enumerate((pl.ds(0, 256), pl.ds(256, 128))):
            for copy in copies[2 * part:2 * part + 2]:
                copy.wait()
            got = got + contract(xr1_far[ab, :, cols], own_rows(xl1_far.at[ab, :, :, cols]))
        for it in range(3):
            mixed[it] = got[:, it * 128:(it + 1) * 128].astype(BF16)

    def send_back(p, ab, n):
        some = pl.ds(*RET[p][ab][n])
        send_all(
            lambda d: ret.at[ab, d, some], (mix0, mix1)[p].at[ab, some, me],
            ret_send.at[p, ab, n], ret_recv.at[p, ab, n],
        )

    def give_back(p, ab):
        for it in range(2):
            ret[ab, it * 32:(it + 1) * 32, 0:12] = mixed[it].reshape(32, 12, 2, 128)
        parts = list(enumerate(RET[p][ab]))
        for n, (first, count) in parts:
            if first + count <= 12:
                send_back(p, ab, n)
        x2[...] = mixed[2].reshape(32, 2, 6, 2, 128)
        top = x2[:, 0].reshape(384, 128).astype(F32)
        bot = pltpu.roll(x2[:, 1].reshape(384, 128).astype(F32), 64, 1)
        ret[ab, 0:32, 12:18] = pick(top, bot).astype(BF16).reshape(32, 6, 2, 128)
        ret[ab, 32:64, 12:18] = pick(bot, top).astype(BF16).reshape(32, 6, 2, 128)
        for n, (first, count) in parts:
            if first + count > 12:
                send_back(p, ab, n)

    def wait_back(p, ab, n):
        wait_bytes((mix0, mix1)[p].at[ab, pl.ds(*RET[p][ab][n])], ret_recv.at[p, ab, n])

    def wait_back_sent(p):
        for ab in range(2):
            for n in range(len(RET[p][ab])):
                wait_bytes(ret.at[ab, pl.ds(0, CHIPS - 1), pl.ds(*RET[p][ab][n])], ret_send.at[p, ab, n])

    def mean_rows(values):
        total = jnp.sum(values.reshape(32, 8, 128), 0)
        total = total + pltpu.roll(total, 4, 0)
        total = total + pltpu.roll(total, 2, 0)
        return (total * (1.0 / C)).reshape(1, 8, 128)

    def norm_mix(values, gain):
        centered = values.reshape(32, 8, 128) - mean_rows(values)
        variance = mean_rows(centered * centered)
        return (centered * lax.rsqrt(variance + 1e-05)).reshape(256, 128) * gain

    def finish(p, u):
        mix = (mix0, mix1)[p]
        cols = []
        for e in range(2):
            vals = jnp.concatenate([mix[ab, 2 * u + e].reshape(128, 128) for ab in range(2)], 0).astype(F32)
            cols.append(norm_mix(vals, gain_out[p]).astype(BF16))
        got = jnp.dot(out_a[p], jnp.concatenate(cols, 1), preferred_element_type=F32)
        for e in range(2):
            tp = 2 * u + e
            zt[tp] = (zt[tp].astype(F32) + gate[tp] * got[:, e * 128:(e + 1) * 128]).astype(BF16)

    def contract_pass(p, mix):
        def second(part):
            wait_channel(p, 1, part, part + 1)
            if part == 0:
                give_back(p, 0)

        cut = len(FWD[p][0]) - 1
        mix(0, lambda part: wait_channel(p, 0, cut * part, cut + part))
        mix(1, second)
        give_back(p, 1)

    weights[0].wait()
    weights[1].wait()
    prepare_in(0)
    for g in range(3):
        if g != 1:
            part = g // 2
            loads[part].wait()
            rows = slice(*((0, 3072), (3072, 4608))[part])
            work[rows] = pbuf[rows].astype(F32)

        @pl.loop(3 * g, 3 * g + 3)
        def _(u):
            for e in range(2):
                load_tiles(2 * u + e, g == 2)
            project(0, u)

        if g == 0:
            pl.semaphore_wait(barrier, CHIPS)
        send_group(0, 0, g)
    send_all_b(0)
    for load in weights[2:]:
        load.wait()
    prepare_out(0)
    gates(0)
    prepare_in(1)
    prepare_out(1)
    contract_pass(0, mix_out)
    wait_sent(0)
    wait_back(0, 0, 0)
    waited = 0
    for g, (start, some) in enumerate(FWD[1][0]):
        while waited < len(RET[0][1]) and RET[0][1][waited][0] < start + some:
            wait_back(0, 1, waited)
            waited += 1

        @pl.loop(start // 2, (start + some) // 2)
        def _(u):
            finish(0, u)
            project(1, u)

        send_group(1, 0, g)
    send_all_b(1)
    gates(1)
    wait_back_sent(0)
    contract_pass(1, mix_in)
    wait_sent(1)
    wait_back(1, 0, 0)
    for g, (start, some) in enumerate(RET[1][1]):
        wait_back(1, 1, g)

        @pl.loop(start // 2, (start + some) // 2)
        def _(u):
            finish(1, u)
            for e in range(2):
                store_tiles(2 * u + e, start >= 12)

        if start + some in (12, 18):
            rows = slice(0, 3072) if start < 12 else slice(3072, 4608)
            out[rows] = work[rows].astype(BF16)
    wait_back_sent(1)


def on_device(pair, norm_in, proj_weight, gate_weight, norm_out, out_weight):
    vmem = pl.BlockSpec(memory_space=pltpu.VMEM)
    hbm = pl.BlockSpec(memory_space=pl.ANY)
    updated = pl.pallas_call(
        kernel,
        out_shape=pltpu.VMEM((ROWS * COLS, C), BF16),
        in_specs=[hbm] * 6,
        out_specs=vmem,
        scratch_shapes=[
            pltpu.VMEM((2, 128), F32),
            pltpu.VMEM((2, 128, 512), BF16),
            pltpu.VMEM((2, 128, 128), BF16),
            pltpu.VMEM((2, 128), F32),
            pltpu.VMEM((2, 128, 128), BF16),
            pltpu.VMEM((ROWS * COLS, C), BF16),
            pltpu.VMEM((PAIRS, 256, 128), BF16),
            pltpu.VMEM((PAIRS, 256, 128), BF16),
            pltpu.VMEM((PAIRS, 256, 128), F32),
            pltpu.VMEM((4, PAIRS, CHIPS, 2, 128), BF16),
            pltpu.VMEM((4, CHIPS, PAIRS, 2, 128), BF16),
            pltpu.VMEM((4, CHIPS, PAIRS, 2, 128), BF16),
            pltpu.VMEM((2, TOKENS, 384), BF16),
            pltpu.VMEM((2, 384, TOKENS), BF16),
            pltpu.VMEM((2, 384, TOKENS), BF16),
            pltpu.VMEM((2, 2, 2, 192, 384), BF16),
            pltpu.VMEM((2, TOKENS, 384), BF16),
            pltpu.VMEM((2, 2, 192, 384), BF16),
            pltpu.VMEM((2, TOKENS, 384), BF16),
            pltpu.VMEM((3, TOKENS, 128), BF16),
            pltpu.VMEM((2, CHIPS, PAIRS, 2, 128), BF16),
            pltpu.VMEM((2, PAIRS, CHIPS, 2, 128), BF16),
            pltpu.VMEM((2, PAIRS, CHIPS, 2, 128), BF16),
            pltpu.VMEM((ROWS * COLS, 128), F32),
            pltpu.VMEM((1024, 128), F32),
            pltpu.VMEM((1024, 128), F32),
            pltpu.VMEM((2, 1024, 256), BF16),
            pltpu.VMEM((2, 256, 256), BF16),
            pltpu.VMEM((2, 256, 256), BF16),
            pltpu.VMEM((2, 128, 128), F32),
            pltpu.VMEM((2, 256, 128), F32),
            pltpu.VMEM((32, 2, 6, 2, 128), BF16),
            pltpu.SemaphoreType.DMA((2, 2, 4)),
            pltpu.SemaphoreType.DMA((2, 2, 4)),
            pltpu.SemaphoreType.DMA((2, 2, 4)),
            pltpu.SemaphoreType.DMA((2, 2, 4)),
            pltpu.SemaphoreType.DMA((12,)),
            pltpu.SemaphoreType.DMA((12,)),
            pltpu.SemaphoreType.DMA((7,)),
        ],
        compiler_params=pltpu.CompilerParams(
            collective_id=0, has_side_effects=True, vmem_limit_bytes=60 * 2**20
        ),
    )(pair.reshape(ROWS * COLS, C), norm_in, proj_weight, gate_weight, norm_out, out_weight)
    return updated.reshape(ROWS, COLS, C)


def solution(mesh):
    placed = (P("row", "col", None), P(), P(), P(), P(), P())
    return jax.shard_map(
        on_device, mesh=mesh, in_specs=placed, out_specs=P("row", "col", None), check_vma=False
    )
```

```python
import functools

import jax
import jax.numpy as jnp
from jax import lax
from jax.experimental import pallas as pl
from jax.experimental.pallas import tpu as pltpu
from jax.sharding import PartitionSpec as P

F32, BF16 = jnp.float32, jnp.bfloat16
MESH = pl.DeviceIdType.MESH

ROWS, COLS, C = 192, 24, 128
CHIPS = 64
PAIRS = 18
THIRDS = ((0, 6), (6, 6), (12, 6))
FWD = ((THIRDS, ((0, 12), (12, 6))), (((0, 2), (2, 4), (6, 6), (12, 6)), ((0, 12), (12, 6))))
RET = ((((0, 18),), ((0, 2), (2, 4), (6, 6), (12, 6))), (((0, 18),), THIRDS))
TOKENS = 768


def chip_coords():
    row, col = lax.axis_index("row"), lax.axis_index("col")
    return col // 8, (row // 2) * 2 + col % 2, (col // 2) % 4, row % 2


def norm_cols(values, gain):
    mean = jnp.mean(values, 0, keepdims=True)
    centered = values - mean
    variance = jnp.mean(centered * centered, 0, keepdims=True)
    return centered * lax.rsqrt(variance + 1e-05) * gain


def sigmoid(values):
    return 0.5 * jnp.tanh(0.5 * values) + 0.5


def kernel(
    pair, norm_in_hbm, proj_hbm, gate_hbm, norm_out_hbm, out_hbm, out,
    norm_in, proj_w, gate_w, norm_out, out_w,
    pbuf, zt, nb, gate, msg, left_right0, left_right1, xl0, xt0, xt0_far, xl1, xr1, xl1_far, xr1_far, mixed, ret, mix0, mix1,
    work, wfa, wfb, proj_a, gate_a, out_a, gain_in, gain_out, x2,
    fwd_send, fwd_recv, ret_send, ret_recv, core_send, core_recv, local,
):
    x, y, z, core = chip_coords()
    y_hi = y // 2
    col = lax.axis_index("col")
    me = y_hi * 32 + col
    sibling = (y_hi * 2 + 1 - core, col)
    y_of = [lax.rem(y + b, 4) for b in range(4)]
    row_of = [v // 2 for v in y_of]
    low_of = [lax.rem(v, 2) for v in y_of]
    z_of = [lax.rem(z + c, 4) * 2 for c in range(4)]

    def pick(a, b):
        return jnp.where(lax.broadcasted_iota(jnp.int32, a.shape, 1) < 64, a, b)

    def each_peer(act):
        @pl.loop(0, 4)
        def _(i):
            for n in range(16):
                b, c = n % 4, (n // 4 + n) % 4
                px = lax.rem(x + (b + c) % 4 + i, 4) * 8

                def one():
                    act(row_of[b], px + low_of[b] + z_of[c])

                if n == 0:
                    pl.when(i > 0)(one)
                else:
                    one()

    def send_all(src_of, dst, send, recv):
        def one(py, pc):
            pltpu.make_async_remote_copy(
                src_ref=src_of(py * 32 + pc), dst_ref=dst, send_sem=send, recv_sem=recv,
                device_id=(py * 2 + core, pc), device_id_type=MESH,
            ).start()

        each_peer(one)
        pltpu.make_async_copy(src_of(me), dst, recv).start()

    def wait_bytes(ref, sem):
        pltpu.make_async_copy(ref, ref, sem).wait()

    barrier = pltpu.get_barrier_semaphore()
    pl.semaphore_signal(barrier, inc=1, device_id=sibling, device_id_type=MESH)
    each_peer(lambda py, pc: pl.semaphore_signal(
        barrier, inc=1, device_id=(py * 2 + core, pc), device_id_type=MESH))

    loads = [
        pltpu.make_async_copy(pair.at[pl.ds(a, n)], pbuf.at[pl.ds(a, n)], local.at[i])
        for i, (a, n) in enumerate(((0, 3072), (3072, 1536)))
    ]
    weights = [
        pltpu.make_async_copy(src, dst, local.at[2 + i])
        for i, (src, dst) in enumerate((
            (norm_in_hbm, norm_in), (proj_hbm, proj_w), (gate_hbm, gate_w), (norm_out_hbm, norm_out), (out_hbm, out_w)))
    ]
    for load in weights[:2] + loads + weights[2:]:
        load.start()

    def picked_gain(ref, p):
        rows = lax.broadcasted_iota(jnp.int32, (2, 128), 0) == p
        row = jnp.sum(jnp.where(rows, ref[...], 0.0), 0, keepdims=True)
        return jnp.broadcast_to(row, (128, 128)).T

    def prepare_in(p):
        wt = proj_w[p].astype(F32).T
        wfa[pl.ds(0, 512, stride=2), :] = wt
        wfa[pl.ds(1, 512, stride=2), :] = jnp.zeros_like(wt)
        wfb[pl.ds(0, 512, stride=2), :] = jnp.zeros_like(wt)
        wfb[pl.ds(1, 512, stride=2), :] = wt
        proj_a[p, :, 0:128] = wfa[...].astype(BF16)
        proj_a[p, :, 128:256] = wfb[...].astype(BF16)
        gain_in[p] = picked_gain(norm_in, p)

    def prepare_out(p):
        gt = gate_w[p].astype(F32).T.astype(BF16)
        zero = jnp.zeros((128, 128), BF16)
        gate_a[p, 0:128, 0:128] = gt
        gate_a[p, 0:128, 128:256] = zero
        gate_a[p, 128:256, 0:128] = zero
        gate_a[p, 128:256, 128:256] = gt
        ow = out_w[p].astype(F32)
        for e in range(2):
            wfa[pl.ds(e, 128, stride=2), :] = ow
            wfa[pl.ds(1 - e, 128, stride=2), :] = jnp.zeros_like(ow)
            out_a[p, e * 128:(e + 1) * 128] = wfa[0:256].T.astype(BF16)
        gain = picked_gain(norm_out, p)
        for e in range(2):
            wfa[pl.ds(e, 128, stride=2), :] = gain
        gain_out[p] = wfa[0:256]

    def half_rows(m, first):
        return pl.ds(128 * 24 + m + 12 * first, 64, stride=24)

    def load_tiles(tp, mixed):
        for e in range(2):
            if mixed:
                m = 2 * tp + e - 24
                vals = jnp.concatenate([work[half_rows(m, y_hi), :], work[half_rows(m, 1 - y_hi), :]], 0)
            else:
                vals = work[pl.ds(2 * tp + e, 128, stride=24), :]
            zt[tp, e * 128:(e + 1) * 128] = vals.T.astype(BF16)

    def store_tiles(tp, mixed):
        for e in range(2):
            vals = zt[tp, e * 128:(e + 1) * 128].astype(F32).T
            if mixed:
                m = 2 * tp + e - 24
                work[half_rows(m, y_hi), :] = vals[0:64]
                work[half_rows(m, 1 - y_hi), :] = vals[64:128]
            else:
                work[pl.ds(2 * tp + e, 128, stride=24), :] = vals

    def project(p, u):
        for e in range(2):
            tp = 2 * u + e
            for h in range(2):
                rows = slice(h * 128, (h + 1) * 128)
                nb[tp, rows] = norm_cols(zt[tp, rows].astype(F32), gain_in[p]).astype(BF16)
        n = jnp.concatenate([nb[2 * u], nb[2 * u + 1]], 1)
        for side in range(2):
            a = proj_a[p, side * 512:(side + 1) * 512]
            got = jnp.dot(a, n, preferred_element_type=F32)
            val = (sigmoid(got[256:512]) * got[0:256]).astype(BF16)
            for ab in range(2):
                for e in range(2):
                    block = val[ab * 128:(ab + 1) * 128, e * 128:(e + 1) * 128]
                    msg[ab * 2 + side, 2 * u + e] = block.reshape(64, 2, 128)

    def gates(p):
        @pl.loop(0, 9)
        def _(u):
            n = jnp.concatenate([nb[2 * u], nb[2 * u + 1]], 1)
            g = sigmoid(jnp.dot(gate_a[p], n, preferred_element_type=F32))
            gate[2 * u] = g[:, 0:128]
            gate[2 * u + 1] = g[:, 128:256]

    def span(p, ab, n):
        return pl.ds(*FWD[p][ab][n])

    def send_group(p, ab, n):
        arrived = (left_right0, left_right1)[p]
        both = pl.ds(2 * ab, 2)
        send_all(
            lambda d: msg.at[both, span(p, ab, n), d], arrived.at[both, me, span(p, ab, n)],
            fwd_send.at[p, ab, n], fwd_recv.at[p, ab, n],
        )

    def send_all_b(p):
        for n in range(len(FWD[p][1])):
            send_group(p, 1, n)

    def wait_channel(p, ab, first=0, last=4):
        arrived = (left_right0, left_right1)[p]
        for n in range(len(FWD[p][ab]))[first:last]:
            wait_bytes(arrived.at[pl.ds(2 * ab, 2), :, span(p, ab, n)], fwd_recv.at[p, ab, n])

    def wait_sent(p):
        for ab in range(2):
            for n in range(len(FWD[p][ab])):
                wait_bytes(
                    msg.at[pl.ds(2 * ab, 2), span(p, ab, n), pl.ds(0, CHIPS - 1)], fwd_send.at[p, ab, n])

    def main_cols(src, i, it):
        return src[i, 32 * it:32 * (it + 1), 0:12].reshape(768, 128)

    def mixed_cols(src, i):
        t = src[i, 0:32, 12:18].reshape(384, 128).astype(F32)
        v = src[i, 32:64, 12:18].reshape(384, 128).astype(F32)
        x2[:, 0] = pick(t, v).astype(BF16).reshape(32, 6, 2, 128)
        x2[:, 1] = pltpu.roll(pick(v, t), 64, 1).astype(BF16).reshape(32, 6, 2, 128)
        return x2[...].reshape(768, 128)

    def columns(src, i, tile):
        return main_cols(src, i, tile) if tile < 2 else mixed_cols(src, i)

    def core_copy(src, dst, i):
        return pltpu.make_async_remote_copy(
            src_ref=src, dst_ref=dst, send_sem=core_send.at[i], recv_sem=core_recv.at[i],
            device_id=sibling, device_id_type=MESH,
        )

    def mix_out(ab, arrive):
        src = left_right0
        copies = []

        def contract(right, owner, tiles, its):
            first = pl.multiple_of(owner * 192, 64)
            rows = slice(tiles[0] * 128, (tiles[-1] + 1) * 128)
            cols = slice(its[0] * 128, (its[-1] + 1) * 128)
            got = jnp.dot(right[ab, rows], xl0[ab, :, cols], preferred_element_type=F32)
            for i, it in enumerate(its):
                for n, tile in enumerate(tiles):
                    piece = got[n * 128:(n + 1) * 128, i * 128:(i + 1) * 128].astype(BF16)
                    if tile < 2:
                        mixed[it, pl.ds(first + 384 * tile, 128), :] = piece
                    else:
                        mixed[it, pl.ds(first + 128, 64), :] = piece[0:64]
                        mixed[it, pl.ds(first + 512, 64), :] = piece[64:128]

        for part, cols in enumerate((slice(0, 256), slice(256, 384))):
            arrive(part)
            for at in range(cols.start, cols.stop, 128):
                xt0[ab, at:at + 128] = columns(src, ab * 2 + 1, at // 128).T
            rows = pl.ds(cols.start, cols.stop - cols.start)
            copy = core_copy(xt0.at[ab, rows], xt0_far.at[ab, rows], 2 * ab + part)
            copy.start()
            copies.append(copy)
            for at in range(cols.start, cols.stop, 128):
                xl0[ab, :, at:at + 128] = columns(src, ab * 2, at // 128)
            if part == 0:
                contract(xt0, core, (0, 1), (0, 1))
                copy.wait()
                contract(xt0_far, 1 - core, (0, 1), (0, 1))

        contract(xt0, core, (2,), (0, 1, 2))
        contract(xt0, core, (0, 1), (2,))
        contract(xt0_far, 1 - core, (0, 1), (2,))
        copies[1].wait()
        contract(xt0_far, 1 - core, (2,), (0, 1, 2))

    def own_rows(ref):
        return jnp.concatenate([ref[0, 0:128], ref[1, 0:128], ref[0, 128:192], ref[1, 128:192]], 0)

    def mix_in(ab, arrive):
        src = left_right1

        def contract(right, left):
            return lax.dot_general(right, left, (((1,), (1,)), ((), ())), preferred_element_type=F32)

        for part, (first, count) in enumerate(((0, 256), (256, 128))):
            arrive(part)
            cols = pl.ds(first, count)
            for at in range(first, first + count, 128):
                xr1[ab, :, at:at + 128] = columns(src, ab * 2 + 1, at // 128)
            right = core_copy(xr1.at[ab, :, cols], xr1_far.at[ab, :, cols], 4 + 4 * ab + 2 * part)
            right.start()
            for at in range(first, first + count, 128):
                xl1[ab, :, :, :, at:at + 128] = columns(src, ab * 2, at // 128).reshape(2, 2, 192, 128)
            left = core_copy(
                xl1.at[ab, :, 1 - core, :, cols], xl1_far.at[ab, :, :, cols], 5 + 4 * ab + 2 * part)
            left.start()
            own = contract(xr1[ab, :, cols], own_rows(xl1.at[ab, :, core, :, cols]))
            got = own if part == 0 else got + own
            right.wait()
            left.wait()
            got = got + contract(xr1_far[ab, :, cols], own_rows(xl1_far.at[ab, :, :, cols]))

        for it in range(3):
            mixed[it] = got[:, it * 128:(it + 1) * 128].astype(BF16)

    def send_back(p, ab, n):
        some = pl.ds(*RET[p][ab][n])
        send_all(
            lambda d: ret.at[ab, d, some], (mix0, mix1)[p].at[ab, some, me],
            ret_send.at[p, ab, n], ret_recv.at[p, ab, n],
        )

    def give_back(p, ab):
        for it in range(2):
            ret[ab, it * 32:(it + 1) * 32, 0:12] = mixed[it].reshape(32, 12, 2, 128)
        parts = list(enumerate(RET[p][ab]))
        for n, (first, count) in parts:
            if first + count <= 12:
                send_back(p, ab, n)
        x2[...] = mixed[2].reshape(32, 2, 6, 2, 128)
        top = x2[:, 0].reshape(384, 128).astype(F32)
        bot = pltpu.roll(x2[:, 1].reshape(384, 128).astype(F32), 64, 1)
        ret[ab, 0:32, 12:18] = pick(top, bot).astype(BF16).reshape(32, 6, 2, 128)
        ret[ab, 32:64, 12:18] = pick(bot, top).astype(BF16).reshape(32, 6, 2, 128)
        for n, (first, count) in parts:
            if first + count > 12:
                send_back(p, ab, n)

    def wait_back(p, ab, n):
        wait_bytes((mix0, mix1)[p].at[ab, pl.ds(*RET[p][ab][n])], ret_recv.at[p, ab, n])

    def wait_back_sent(p):
        for ab in range(2):
            for n in range(len(RET[p][ab])):
                wait_bytes(ret.at[ab, pl.ds(0, CHIPS - 1), pl.ds(*RET[p][ab][n])], ret_send.at[p, ab, n])

    def mean_rows(values):
        total = jnp.sum(values.reshape(32, 8, 128), 0)
        total = total + pltpu.roll(total, 4, 0)
        total = total + pltpu.roll(total, 2, 0)
        return (total * (1.0 / C)).reshape(1, 8, 128)

    def norm_mix(values, gain):
        centered = values.reshape(32, 8, 128) - mean_rows(values)
        variance = mean_rows(centered * centered)
        return (centered * lax.rsqrt(variance + 1e-05)).reshape(256, 128) * gain

    def finish(p, u):
        mix = (mix0, mix1)[p]
        cols = []
        for e in range(2):
            vals = jnp.concatenate([mix[ab, 2 * u + e].reshape(128, 128) for ab in range(2)], 0).astype(F32)
            cols.append(norm_mix(vals, gain_out[p]).astype(BF16))
        got = jnp.dot(out_a[p], jnp.concatenate(cols, 1), preferred_element_type=F32)
        for e in range(2):
            tp = 2 * u + e
            zt[tp] = (zt[tp].astype(F32) + gate[tp] * got[:, e * 128:(e + 1) * 128]).astype(BF16)

    def contract_pass(p, mix):
        def second(part):
            wait_channel(p, 1, part, part + 1)
            if part == 0:
                give_back(p, 0)

        cut = len(FWD[p][0]) - 1
        mix(0, lambda part: wait_channel(p, 0, cut * part, cut + part))
        mix(1, second)
        give_back(p, 1)

    weights[0].wait()
    weights[1].wait()
    prepare_in(0)
    for g in range(3):
        if g != 1:
            part = g // 2
            loads[part].wait()
            rows = slice(*((0, 3072), (3072, 4608))[part])
            work[rows] = pbuf[rows].astype(F32)

        @pl.loop(3 * g, 3 * g + 3)
        def _(u):
            for e in range(2):
                load_tiles(2 * u + e, g == 2)
            project(0, u)

        if g == 0:
            pl.semaphore_wait(barrier, CHIPS)
        send_group(0, 0, g)
    send_all_b(0)
    for load in weights[2:]:
        load.wait()
    prepare_out(0)
    gates(0)
    prepare_in(1)
    prepare_out(1)
    contract_pass(0, mix_out)
    wait_sent(0)
    wait_back(0, 0, 0)
    waited = 0
    for g, (start, some) in enumerate(FWD[1][0]):
        while waited < len(RET[0][1]) and RET[0][1][waited][0] < start + some:
            wait_back(0, 1, waited)
            waited += 1

        @pl.loop(start // 2, (start + some) // 2)
        def _(u):
            finish(0, u)
            project(1, u)

        send_group(1, 0, g)
    send_all_b(1)
    gates(1)
    wait_back_sent(0)
    contract_pass(1, mix_in)
    wait_sent(1)
    wait_back(1, 0, 0)
    for g, (start, some) in enumerate(RET[1][1]):
        wait_back(1, 1, g)

        @pl.loop(start // 2, (start + some) // 2)
        def _(u):
            finish(1, u)
            for e in range(2):
                store_tiles(2 * u + e, start >= 12)

        if start + some in (12, 18):
            rows = slice(0, 3072) if start < 12 else slice(3072, 4608)
            out[rows] = work[rows].astype(BF16)
    wait_back_sent(1)


def on_device(pair, norm_in, proj_weight, gate_weight, norm_out, out_weight):
    vmem = pl.BlockSpec(memory_space=pltpu.VMEM)
    hbm = pl.BlockSpec(memory_space=pl.ANY)
    updated = pl.pallas_call(
        kernel,
        out_shape=pltpu.VMEM((ROWS * COLS, C), BF16),
        in_specs=[hbm] * 6,
        out_specs=vmem,
        scratch_shapes=[
            pltpu.VMEM((2, 128), F32),
            pltpu.VMEM((2, 128, 512), BF16),
            pltpu.VMEM((2, 128, 128), BF16),
            pltpu.VMEM((2, 128), F32),
            pltpu.VMEM((2, 128, 128), BF16),
            pltpu.VMEM((ROWS * COLS, C), BF16),
            pltpu.VMEM((PAIRS, 256, 128), BF16),
            pltpu.VMEM((PAIRS, 256, 128), BF16),
            pltpu.VMEM((PAIRS, 256, 128), F32),
            pltpu.VMEM((4, PAIRS, CHIPS, 2, 128), BF16),
            pltpu.VMEM((4, CHIPS, PAIRS, 2, 128), BF16),
            pltpu.VMEM((4, CHIPS, PAIRS, 2, 128), BF16),
            pltpu.VMEM((2, TOKENS, 384), BF16),
            pltpu.VMEM((2, 384, TOKENS), BF16),
            pltpu.VMEM((2, 384, TOKENS), BF16),
            pltpu.VMEM((2, 2, 2, 192, 384), BF16),
            pltpu.VMEM((2, TOKENS, 384), BF16),
            pltpu.VMEM((2, 2, 192, 384), BF16),
            pltpu.VMEM((2, TOKENS, 384), BF16),
            pltpu.VMEM((3, TOKENS, 128), BF16),
            pltpu.VMEM((2, CHIPS, PAIRS, 2, 128), BF16),
            pltpu.VMEM((2, PAIRS, CHIPS, 2, 128), BF16),
            pltpu.VMEM((2, PAIRS, CHIPS, 2, 128), BF16),
            pltpu.VMEM((ROWS * COLS, 128), F32),
            pltpu.VMEM((1024, 128), F32),
            pltpu.VMEM((1024, 128), F32),
            pltpu.VMEM((2, 1024, 256), BF16),
            pltpu.VMEM((2, 256, 256), BF16),
            pltpu.VMEM((2, 256, 256), BF16),
            pltpu.VMEM((2, 128, 128), F32),
            pltpu.VMEM((2, 256, 128), F32),
            pltpu.VMEM((32, 2, 6, 2, 128), BF16),
            pltpu.SemaphoreType.DMA((2, 2, 4)),
            pltpu.SemaphoreType.DMA((2, 2, 4)),
            pltpu.SemaphoreType.DMA((2, 2, 4)),
            pltpu.SemaphoreType.DMA((2, 2, 4)),
            pltpu.SemaphoreType.DMA((12,)),
            pltpu.SemaphoreType.DMA((12,)),
            pltpu.SemaphoreType.DMA((7,)),
        ],
        compiler_params=pltpu.CompilerParams(
            collective_id=0, has_side_effects=True, vmem_limit_bytes=60 * 2**20
        ),
    )(pair.reshape(ROWS * COLS, C), norm_in, proj_weight, gate_weight, norm_out, out_weight)
    return updated.reshape(ROWS, COLS, C)


def solution(mesh):
    placed = (P("row", "col", None), P(), P(), P(), P(), P())
    return jax.shard_map(
        on_device, mesh=mesh, in_specs=placed, out_specs=P("row", "col", None), check_vma=False
    )
```

```python
import functools

import jax
import jax.numpy as jnp
from jax import lax
from jax.experimental import pallas as pl
from jax.experimental.pallas import tpu as pltpu
from jax.sharding import PartitionSpec as P

F32, BF16 = jnp.float32, jnp.bfloat16
MESH = pl.DeviceIdType.MESH

ROWS, COLS, C = 192, 24, 128
CHIPS = 64
PAIRS = 18
THIRDS = ((0, 6), (6, 6), (12, 6))
FWD = ((THIRDS, ((0, 12), (12, 6))), (((0, 2), (2, 4), (6, 6), (12, 6)), ((0, 12), (12, 6))))
RET = ((((0, 18),), ((0, 2), (2, 4), (6, 6), (12, 6))), (((0, 18),), THIRDS))
TOKENS = 768


def chip_coords():
    row, col = lax.axis_index("row"), lax.axis_index("col")
    return col // 8, (row // 2) * 2 + col % 2, (col // 2) % 4, row % 2


def norm_cols(values, gain):
    mean = jnp.mean(values, 0, keepdims=True)
    centered = values - mean
    variance = jnp.mean(centered * centered, 0, keepdims=True)
    return centered * lax.rsqrt(variance + 1e-05) * gain


def sigmoid(values):
    return 0.5 * jnp.tanh(0.5 * values) + 0.5


def kernel(
    pair, norm_in_hbm, proj_hbm, gate_hbm, norm_out_hbm, out_hbm, out,
    norm_in, proj_w, gate_w, norm_out, out_w,
    pbuf, zt, nb, gate, msg, left_right0, left_right1, xl0, xt0, xt0_far, xl1, xr1, xl1_far, xr1_far, mixed, ret, mix0, mix1,
    work, wfa, wfb, proj_a, gate_a, out_a, gain_in, gain_out, x2,
    fwd_send, fwd_recv, ret_send, ret_recv, core_send, core_recv, local,
):
    x, y, z, core = chip_coords()
    y_hi = y // 2
    col = lax.axis_index("col")
    me = y_hi * 32 + col
    sibling = (y_hi * 2 + 1 - core, col)
    y_of = [lax.rem(y + b, 4) for b in range(4)]
    row_of = [v // 2 for v in y_of]
    low_of = [lax.rem(v, 2) for v in y_of]
    z_of = [lax.rem(z + c, 4) * 2 for c in range(4)]

    def pick(a, b):
        return jnp.where(lax.broadcasted_iota(jnp.int32, a.shape, 1) < 64, a, b)

    def each_peer(act):
        @pl.loop(0, 4)
        def _(i):
            for n in range(16):
                b, c = n % 4, (n // 4 + n) % 4
                px = lax.rem(x + (b + c) % 4 + i, 4) * 8

                def one():
                    act(row_of[b], px + low_of[b] + z_of[c])

                if n == 0:
                    pl.when(i > 0)(one)
                else:
                    one()

    def send_all(src_of, dst, send, recv):
        def one(py, pc):
            pltpu.make_async_remote_copy(
                src_ref=src_of(py * 32 + pc), dst_ref=dst, send_sem=send, recv_sem=recv,
                device_id=(py * 2 + core, pc), device_id_type=MESH,
            ).start()

        each_peer(one)
        pltpu.make_async_copy(src_of(me), dst, recv).start()

    def wait_bytes(ref, sem):
        pltpu.make_async_copy(ref, ref, sem).wait()

    barrier = pltpu.get_barrier_semaphore()
    pl.semaphore_signal(barrier, inc=1, device_id=sibling, device_id_type=MESH)
    each_peer(lambda py, pc: pl.semaphore_signal(
        barrier, inc=1, device_id=(py * 2 + core, pc), device_id_type=MESH))

    loads = [
        pltpu.make_async_copy(pair.at[pl.ds(a, n)], pbuf.at[pl.ds(a, n)], local.at[i])
        for i, (a, n) in enumerate(((0, 3072), (3072, 1536)))
    ]
    weights = [
        pltpu.make_async_copy(src, dst, local.at[2 + i])
        for i, (src, dst) in enumerate((
            (norm_in_hbm, norm_in), (proj_hbm, proj_w), (gate_hbm, gate_w), (norm_out_hbm, norm_out), (out_hbm, out_w)))
    ]
    for load in weights[:2] + loads + weights[2:]:
        load.start()

    def picked_gain(ref, p):
        rows = lax.broadcasted_iota(jnp.int32, (2, 128), 0) == p
        row = jnp.sum(jnp.where(rows, ref[...], 0.0), 0, keepdims=True)
        return jnp.broadcast_to(row, (128, 128)).T

    def prepare_in(p):
        wt = proj_w[p].astype(F32).T
        wfa[pl.ds(0, 512, stride=2), :] = wt
        wfa[pl.ds(1, 512, stride=2), :] = jnp.zeros_like(wt)
        wfb[pl.ds(0, 512, stride=2), :] = jnp.zeros_like(wt)
        wfb[pl.ds(1, 512, stride=2), :] = wt
        proj_a[p, :, 0:128] = wfa[...].astype(BF16)
        proj_a[p, :, 128:256] = wfb[...].astype(BF16)
        gain_in[p] = picked_gain(norm_in, p)

    def prepare_out(p):
        gt = gate_w[p].astype(F32).T.astype(BF16)
        zero = jnp.zeros((128, 128), BF16)
        gate_a[p, 0:128, 0:128] = gt
        gate_a[p, 0:128, 128:256] = zero
        gate_a[p, 128:256, 0:128] = zero
        gate_a[p, 128:256, 128:256] = gt
        ow = out_w[p].astype(F32)
        for e in range(2):
            wfa[pl.ds(e, 128, stride=2), :] = ow
            wfa[pl.ds(1 - e, 128, stride=2), :] = jnp.zeros_like(ow)
            out_a[p, e * 128:(e + 1) * 128] = wfa[0:256].T.astype(BF16)
        gain = picked_gain(norm_out, p)
        for e in range(2):
            wfa[pl.ds(e, 128, stride=2), :] = gain
        gain_out[p] = wfa[0:256]

    def half_rows(m, first):
        return pl.ds(128 * 24 + m + 12 * first, 64, stride=24)

    def load_tiles(tp, mixed):
        for e in range(2):
            if mixed:
                m = 2 * tp + e - 24
                vals = jnp.concatenate([work[half_rows(m, y_hi), :], work[half_rows(m, 1 - y_hi), :]], 0)
            else:
                vals = work[pl.ds(2 * tp + e, 128, stride=24), :]
            zt[tp, e * 128:(e + 1) * 128] = vals.T.astype(BF16)

    def store_tiles(tp, mixed):
        for e in range(2):
            vals = zt[tp, e * 128:(e + 1) * 128].astype(F32).T
            if mixed:
                m = 2 * tp + e - 24
                work[half_rows(m, y_hi), :] = vals[0:64]
                work[half_rows(m, 1 - y_hi), :] = vals[64:128]
            else:
                work[pl.ds(2 * tp + e, 128, stride=24), :] = vals

    def project(p, u):
        for e in range(2):
            tp = 2 * u + e
            for h in range(2):
                rows = slice(h * 128, (h + 1) * 128)
                nb[tp, rows] = norm_cols(zt[tp, rows].astype(F32), gain_in[p]).astype(BF16)
        n = jnp.concatenate([nb[2 * u], nb[2 * u + 1]], 1)
        for side in range(2):
            a = proj_a[p, side * 512:(side + 1) * 512]
            got = jnp.dot(a, n, preferred_element_type=F32)
            val = (sigmoid(got[256:512]) * got[0:256]).astype(BF16)
            for ab in range(2):
                for e in range(2):
                    block = val[ab * 128:(ab + 1) * 128, e * 128:(e + 1) * 128]
                    msg[ab * 2 + side, 2 * u + e] = block.reshape(64, 2, 128)

    def gates(p):
        @pl.loop(0, 9)
        def _(u):
            n = jnp.concatenate([nb[2 * u], nb[2 * u + 1]], 1)
            g = sigmoid(jnp.dot(gate_a[p], n, preferred_element_type=F32))
            gate[2 * u] = g[:, 0:128]
            gate[2 * u + 1] = g[:, 128:256]

    def span(p, ab, n):
        return pl.ds(*FWD[p][ab][n])

    def send_group(p, ab, n):
        arrived = (left_right0, left_right1)[p]
        both = pl.ds(2 * ab, 2)
        send_all(
            lambda d: msg.at[both, span(p, ab, n), d], arrived.at[both, me, span(p, ab, n)],
            fwd_send.at[p, ab, n], fwd_recv.at[p, ab, n],
        )

    def send_all_b(p):
        for n in range(len(FWD[p][1])):
            send_group(p, 1, n)

    def wait_channel(p, ab, first=0, last=4):
        arrived = (left_right0, left_right1)[p]
        for n in range(len(FWD[p][ab]))[first:last]:
            wait_bytes(arrived.at[pl.ds(2 * ab, 2), :, span(p, ab, n)], fwd_recv.at[p, ab, n])

    def wait_sent(p):
        for ab in range(2):
            for n in range(len(FWD[p][ab])):
                wait_bytes(
                    msg.at[pl.ds(2 * ab, 2), span(p, ab, n), pl.ds(0, CHIPS - 1)], fwd_send.at[p, ab, n])

    def main_cols(src, i, it):
        return src[i, 32 * it:32 * (it + 1), 0:12].reshape(768, 128)

    def mixed_cols(src, i):
        t = src[i, 0:32, 12:18].reshape(384, 128).astype(F32)
        v = src[i, 32:64, 12:18].reshape(384, 128).astype(F32)
        x2[:, 0] = pick(t, v).astype(BF16).reshape(32, 6, 2, 128)
        x2[:, 1] = pltpu.roll(pick(v, t), 64, 1).astype(BF16).reshape(32, 6, 2, 128)
        return x2[...].reshape(768, 128)

    def columns(src, i, tile):
        return main_cols(src, i, tile) if tile < 2 else mixed_cols(src, i)

    def core_copy(src, dst, i):
        return pltpu.make_async_remote_copy(
            src_ref=src, dst_ref=dst, send_sem=core_send.at[i], recv_sem=core_recv.at[i],
            device_id=sibling, device_id_type=MESH,
        )

    def mix_out(ab, arrive):
        src = left_right0
        copies = []
        for part, cols in enumerate((slice(0, 256), slice(256, 384))):
            arrive(part)
            for at in range(cols.start, cols.stop, 128):
                xt0[ab, at:at + 128] = columns(src, ab * 2 + 1, at // 128).T
            rows = pl.ds(cols.start, cols.stop - cols.start)
            copy = core_copy(xt0.at[ab, rows], xt0_far.at[ab, rows], 2 * ab + part)
            copy.start()
            copies.append(copy)
            for at in range(cols.start, cols.stop, 128):
                xl0[ab, :, at:at + 128] = columns(src, ab * 2, at // 128)

        def contract(right, owner, tiles):
            first = pl.multiple_of(owner * 192, 64)
            got = jnp.dot(right[ab, tiles[0] * 128:(tiles[-1] + 1) * 128], xl0[ab], preferred_element_type=F32)
            for it in range(3):
                for n, tile in enumerate(tiles):
                    piece = got[n * 128:(n + 1) * 128, it * 128:(it + 1) * 128].astype(BF16)
                    if tile < 2:
                        mixed[it, pl.ds(first + 384 * tile, 128), :] = piece
                    else:
                        mixed[it, pl.ds(first + 128, 64), :] = piece[0:64]
                        mixed[it, pl.ds(first + 512, 64), :] = piece[64:128]

        contract(xt0, core, (0, 1, 2))
        copies[0].wait()
        contract(xt0_far, 1 - core, (0, 1))
        copies[1].wait()
        contract(xt0_far, 1 - core, (2,))

    def own_rows(ref):
        return jnp.concatenate([ref[0, 0:128], ref[1, 0:128], ref[0, 128:192], ref[1, 128:192]], 0)

    def mix_in(ab, arrive):
        src = left_right1

        def contract(right, left):
            return lax.dot_general(right, left, (((1,), (1,)), ((), ())), preferred_element_type=F32)

        for part, (first, count) in enumerate(((0, 256), (256, 128))):
            arrive(part)
            cols = pl.ds(first, count)
            for at in range(first, first + count, 128):
                xr1[ab, :, at:at + 128] = columns(src, ab * 2 + 1, at // 128)
            right = core_copy(xr1.at[ab, :, cols], xr1_far.at[ab, :, cols], 4 + 4 * ab + 2 * part)
            right.start()
            for at in range(first, first + count, 128):
                xl1[ab, :, :, :, at:at + 128] = columns(src, ab * 2, at // 128).reshape(2, 2, 192, 128)
            left = core_copy(
                xl1.at[ab, :, 1 - core, :, cols], xl1_far.at[ab, :, :, cols], 5 + 4 * ab + 2 * part)
            left.start()
            own = contract(xr1[ab, :, cols], own_rows(xl1.at[ab, :, core, :, cols]))
            got = own if part == 0 else got + own
            right.wait()
            left.wait()
            got = got + contract(xr1_far[ab, :, cols], own_rows(xl1_far.at[ab, :, :, cols]))

        for it in range(3):
            mixed[it] = got[:, it * 128:(it + 1) * 128].astype(BF16)

    def send_back(p, ab, n):
        some = pl.ds(*RET[p][ab][n])
        send_all(
            lambda d: ret.at[ab, d, some], (mix0, mix1)[p].at[ab, some, me],
            ret_send.at[p, ab, n], ret_recv.at[p, ab, n],
        )

    def give_back(p, ab):
        for it in range(2):
            ret[ab, it * 32:(it + 1) * 32, 0:12] = mixed[it].reshape(32, 12, 2, 128)
        parts = list(enumerate(RET[p][ab]))
        for n, (first, count) in parts:
            if first + count <= 12:
                send_back(p, ab, n)
        x2[...] = mixed[2].reshape(32, 2, 6, 2, 128)
        top = x2[:, 0].reshape(384, 128).astype(F32)
        bot = pltpu.roll(x2[:, 1].reshape(384, 128).astype(F32), 64, 1)
        ret[ab, 0:32, 12:18] = pick(top, bot).astype(BF16).reshape(32, 6, 2, 128)
        ret[ab, 32:64, 12:18] = pick(bot, top).astype(BF16).reshape(32, 6, 2, 128)
        for n, (first, count) in parts:
            if first + count > 12:
                send_back(p, ab, n)

    def wait_back(p, ab, n):
        wait_bytes((mix0, mix1)[p].at[ab, pl.ds(*RET[p][ab][n])], ret_recv.at[p, ab, n])

    def wait_back_sent(p):
        for ab in range(2):
            for n in range(len(RET[p][ab])):
                wait_bytes(ret.at[ab, pl.ds(0, CHIPS - 1), pl.ds(*RET[p][ab][n])], ret_send.at[p, ab, n])

    def mean_rows(values):
        total = jnp.sum(values.reshape(32, 8, 128), 0)
        total = total + pltpu.roll(total, 4, 0)
        total = total + pltpu.roll(total, 2, 0)
        return (total * (1.0 / C)).reshape(1, 8, 128)

    def norm_mix(values, gain):
        centered = values.reshape(32, 8, 128) - mean_rows(values)
        variance = mean_rows(centered * centered)
        return (centered * lax.rsqrt(variance + 1e-05)).reshape(256, 128) * gain

    def finish(p, u):
        mix = (mix0, mix1)[p]
        cols = []
        for e in range(2):
            vals = jnp.concatenate([mix[ab, 2 * u + e].reshape(128, 128) for ab in range(2)], 0).astype(F32)
            cols.append(norm_mix(vals, gain_out[p]).astype(BF16))
        got = jnp.dot(out_a[p], jnp.concatenate(cols, 1), preferred_element_type=F32)
        for e in range(2):
            tp = 2 * u + e
            zt[tp] = (zt[tp].astype(F32) + gate[tp] * got[:, e * 128:(e + 1) * 128]).astype(BF16)

    def contract_pass(p, mix):
        def second(part):
            wait_channel(p, 1, part, part + 1)
            if part == 0:
                give_back(p, 0)

        cut = len(FWD[p][0]) - 1
        mix(0, lambda part: wait_channel(p, 0, cut * part, cut + part))
        mix(1, second)
        give_back(p, 1)

    weights[0].wait()
    weights[1].wait()
    prepare_in(0)
    for g in range(3):
        if g != 1:
            part = g // 2
            loads[part].wait()
            rows = slice(*((0, 3072), (3072, 4608))[part])
            work[rows] = pbuf[rows].astype(F32)

        @pl.loop(3 * g, 3 * g + 3)
        def _(u):
            for e in range(2):
                load_tiles(2 * u + e, g == 2)
            project(0, u)

        if g == 0:
            pl.semaphore_wait(barrier, CHIPS)
        send_group(0, 0, g)
    send_all_b(0)
    for load in weights[2:]:
        load.wait()
    prepare_out(0)
    gates(0)
    prepare_in(1)
    prepare_out(1)
    contract_pass(0, mix_out)
    wait_sent(0)
    wait_back(0, 0, 0)
    waited = 0
    for g, (start, some) in enumerate(FWD[1][0]):
        while waited < len(RET[0][1]) and RET[0][1][waited][0] < start + some:
            wait_back(0, 1, waited)
            waited += 1

        @pl.loop(start // 2, (start + some) // 2)
        def _(u):
            finish(0, u)
            project(1, u)

        send_group(1, 0, g)
    send_all_b(1)
    gates(1)
    wait_back_sent(0)
    contract_pass(1, mix_in)
    wait_sent(1)
    wait_back(1, 0, 0)
    for g, (start, some) in enumerate(RET[1][1]):
        wait_back(1, 1, g)

        @pl.loop(start // 2, (start + some) // 2)
        def _(u):
            finish(1, u)
            for e in range(2):
                store_tiles(2 * u + e, start >= 12)

        if start + some in (12, 18):
            rows = slice(0, 3072) if start < 12 else slice(3072, 4608)
            out[rows] = work[rows].astype(BF16)
    wait_back_sent(1)


def on_device(pair, norm_in, proj_weight, gate_weight, norm_out, out_weight):
    vmem = pl.BlockSpec(memory_space=pltpu.VMEM)
    hbm = pl.BlockSpec(memory_space=pl.ANY)
    updated = pl.pallas_call(
        kernel,
        out_shape=pltpu.VMEM((ROWS * COLS, C), BF16),
        in_specs=[hbm] * 6,
        out_specs=vmem,
        scratch_shapes=[
            pltpu.VMEM((2, 128), F32),
            pltpu.VMEM((2, 128, 512), BF16),
            pltpu.VMEM((2, 128, 128), BF16),
            pltpu.VMEM((2, 128), F32),
            pltpu.VMEM((2, 128, 128), BF16),
            pltpu.VMEM((ROWS * COLS, C), BF16),
            pltpu.VMEM((PAIRS, 256, 128), BF16),
            pltpu.VMEM((PAIRS, 256, 128), BF16),
            pltpu.VMEM((PAIRS, 256, 128), F32),
            pltpu.VMEM((4, PAIRS, CHIPS, 2, 128), BF16),
            pltpu.VMEM((4, CHIPS, PAIRS, 2, 128), BF16),
            pltpu.VMEM((4, CHIPS, PAIRS, 2, 128), BF16),
            pltpu.VMEM((2, TOKENS, 384), BF16),
            pltpu.VMEM((2, 384, TOKENS), BF16),
            pltpu.VMEM((2, 384, TOKENS), BF16),
            pltpu.VMEM((2, 2, 2, 192, 384), BF16),
            pltpu.VMEM((2, TOKENS, 384), BF16),
            pltpu.VMEM((2, 2, 192, 384), BF16),
            pltpu.VMEM((2, TOKENS, 384), BF16),
            pltpu.VMEM((3, TOKENS, 128), BF16),
            pltpu.VMEM((2, CHIPS, PAIRS, 2, 128), BF16),
            pltpu.VMEM((2, PAIRS, CHIPS, 2, 128), BF16),
            pltpu.VMEM((2, PAIRS, CHIPS, 2, 128), BF16),
            pltpu.VMEM((ROWS * COLS, 128), F32),
            pltpu.VMEM((1024, 128), F32),
            pltpu.VMEM((1024, 128), F32),
            pltpu.VMEM((2, 1024, 256), BF16),
            pltpu.VMEM((2, 256, 256), BF16),
            pltpu.VMEM((2, 256, 256), BF16),
            pltpu.VMEM((2, 128, 128), F32),
            pltpu.VMEM((2, 256, 128), F32),
            pltpu.VMEM((32, 2, 6, 2, 128), BF16),
            pltpu.SemaphoreType.DMA((2, 2, 4)),
            pltpu.SemaphoreType.DMA((2, 2, 4)),
            pltpu.SemaphoreType.DMA((2, 2, 4)),
            pltpu.SemaphoreType.DMA((2, 2, 4)),
            pltpu.SemaphoreType.DMA((12,)),
            pltpu.SemaphoreType.DMA((12,)),
            pltpu.SemaphoreType.DMA((7,)),
        ],
        compiler_params=pltpu.CompilerParams(
            collective_id=0, has_side_effects=True, vmem_limit_bytes=60 * 2**20
        ),
    )(pair.reshape(ROWS * COLS, C), norm_in, proj_weight, gate_weight, norm_out, out_weight)
    return updated.reshape(ROWS, COLS, C)


def solution(mesh):
    placed = (P("row", "col", None), P(), P(), P(), P(), P())
    return jax.shard_map(
        on_device, mesh=mesh, in_specs=placed, out_specs=P("row", "col", None), check_vma=False
    )
```
